768 devices in a mesh: grp: 96 (over y_lo, z, core), intra: 8 (over y_hi, x).
Axes of the slice: x: 4, y: 8 (y_hi: 2, y_lo: 4; y = y_hi * 4 + y_lo), z: 12, core: 2. Of those that a mesh axis runs over, the one named last changes fastest.
Arguments:
- grads: bfloat16 [768, 192, 2048], P(('grp', 'intra')), may hold values from -4 to 4
- sign_rows: int32 [192, 16], replicated, may hold values from 0 to 1
- sign_cols: int32 [192, 128], replicated, may hold values from 0 to 1
- block_order: int32 [192], replicated, may hold values from 0 to 191, each once
- master: float32 [192, 2048], P('grp'), may hold values from -6 to 6
- first_moment: float32 [192, 2048], P('grp'), may hold values from -6 to 6
- second_moment: float32 [192, 2048], P('grp'), may hold values from 0.5 to 4
Outputs:
- new_master: float32 [192, 2048], P('grp')
- new_first: float32 [192, 2048], P('grp')
- new_second: float32 [192, 2048], P('grp')
- params: bfloat16 [192, 2048], replicated
The draws below stay inside these ranges and needn't reach their ends.
Inputs may be any that keep to these rules, and one draw needn't show every extreme that they name: `block_order`: each block id appears in exactly one slot.
All inputs are finite; a program needn't handle non-finite values.
Results may differ from the reference program's by a relative error of at most 0.0029.
Values may be sent and summed in bfloat16 or wider, within the bound.
No kernel may reach another device: no remote copies, remote signals or barrier semaphores. Data moves between devices by JAX's collectives and lax.ppermute only.
A program may use at most 32 MiB of HBM per device.

```python
import math
import jax
import jax.numpy as jnp
from jax import lax

SUB = 16
LANE = 128
BLOCK = 2048
BLOCKS = 192
DEVICES = 768


def plant(array, rng, least, top_value):
    longest = array.shape.index(max(array.shape))
    spots = []
    for shift in (0, 1):
        where = [jax.random.randint(jax.random.fold_in(rng, axis), (), 0, length) for axis, length in enumerate(array.shape)]
        where[longest] = (where[longest] + shift) % array.shape[longest]
        spots.append(tuple(where))
    return array.at[spots[0]].set(least).at[spots[1]].set(top_value)


def spiked(drawn, rng, source, target, blocks, factor):
    def block_of(position):
        return (jnp.arange(drawn.shape[position]) // (drawn.shape[position] // blocks)).reshape((-1,) + (1,) * (drawn.ndim - 1 - position))

    first = jax.random.permutation(rng, blocks)[block_of(target)]
    second = (block_of(target) + blocks // 2) % blocks
    return jnp.where((block_of(source) == first) | (block_of(source) == second), factor * drawn, drawn)


def shard_levels(rng, dims, shards, low, high):
    def one(position, shards_of):
        draws = jax.random.uniform(jax.random.fold_in(jax.random.fold_in(rng, 6), position), (shards_of,), jnp.float32, low / len(shards), high / len(shards))
        return jnp.repeat(jnp.exp(draws), dims[position] // shards_of).reshape((-1,) + (1,) * (len(dims) - position - 1))

    loudness = one(*shards[0])
    for cut in shards[1:]:
        loudness = loudness * one(*cut)
    return loudness


def centred(own_key, extent, scale, limit, shards=(), held_as=jnp.bfloat16):
    gain = shard_levels(own_key, extent, shards, -0.22, 0.18) if shards else 1.0
    array = jax.random.normal(own_key, extent, jnp.float32) * scale * gain
    return jnp.minimum(jnp.maximum(array, -limit), limit).astype(held_as)


def bell_draw_with(rng, shape, deviation, most, cuts, heavy, dtype=jnp.bfloat16):
    drawn = deviation * jax.random.normal(rng, shape, jnp.float32)
    if cuts:
        drawn = drawn * shard_levels(rng, shape, cuts, -0.22, 0.18)
    return jnp.clip(spiked(drawn, jax.random.fold_in(rng, 3), *heavy), -most, most).astype(dtype)


def setup_inputs(seed: int = 0) -> dict:
    splits = jax.random.split(jax.random.key(seed), 8)
    return {
        "grads": bell_draw_with(splits[0], (DEVICES, BLOCKS, BLOCK), (2.0 / DEVICES ** 0.5), 4.0, ((0, 768),), (0, 1, 192, 6.0)),
        "sign_rows": plant(jax.random.randint(splits[1], (BLOCKS, SUB), 0, 2), jax.random.fold_in(splits[1], 1), 0, 1).astype(jnp.int32),
        "sign_cols": plant(jax.random.randint(splits[2], (BLOCKS, LANE), 0, 2), jax.random.fold_in(splits[2], 1), 0, 1).astype(jnp.int32),
        "block_order": jax.random.permutation(splits[3], BLOCKS).astype(jnp.int32),
        "master": centred(splits[4], (BLOCKS, BLOCK), 1.0, 6.0, ((0, 96),), jnp.float32),
        "first_moment": centred(splits[5], (BLOCKS, BLOCK), 1.0, 6.0, ((0, 96),), jnp.float32),
        "second_moment": jnp.clip(jnp.exp(math.log(4.0) - 2.0794415 * jax.random.uniform(splits[6], (BLOCKS, BLOCK), jnp.float32) ** shard_levels(splits[6], (BLOCKS, BLOCK), ((0, 96),), -0.2, 0.2)), 0.5, 4.0),
    }


beta_one = 0.9
beta_two = 0.95
first_fix = 1.0 - math.exp(100.0 * math.log(0.9))
second_fix = 1.0 - math.exp(100.0 * math.log(0.95))
learn_rate = 0.25
weight_decay = 0.1
epsilon = 1e-08

def walsh_transform(values):
    length = values.shape[-1]
    leading = values.shape[:-1]
    half_span = 1
    while half_span < length:
        split = values.reshape(leading + (length // (2 * half_span), 2, half_span))
        first_half = split[..., 0, :]
        second_half = split[..., 1, :]
        values = jnp.stack([first_half + second_half, first_half - second_half], axis=-2).reshape(leading + (length,))
        half_span = half_span * 2
    return values

def sign_table(picked_rows, picked_cols):
    table = (2 * picked_rows - 1)[:, :, None] * (2 * picked_cols - 1)[:, None, :]
    return table.reshape(picked_rows.shape[0], -1).astype(jnp.float32)

def reference(grads, sign_rows, sign_cols, block_order, master, first_moment, second_moment):
    order = block_order.astype(jnp.int32)
    signs = sign_table(sign_rows[order], sign_cols[order])
    inv_root = 1.0 / math.sqrt(BLOCK)

    def accumulate(running, device_grad):
        slot_rows = device_grad[order].astype(jnp.float32) * signs
        rotated = (walsh_transform(slot_rows) * inv_root).astype(jnp.bfloat16).astype(jnp.float32)
        return (running + rotated, None)
    summed, _ = lax.scan(accumulate, jnp.zeros((BLOCKS, BLOCK), jnp.float32), grads)
    new_first = beta_one * first_moment + (1.0 - beta_one) * summed
    new_second = beta_two * second_moment + (1.0 - beta_two) * summed * summed
    update = new_first / first_fix / (jnp.sqrt(new_second / second_fix) + epsilon)
    restored = walsh_transform(update) * inv_root * signs
    new_master = master - learn_rate * (restored + weight_decay * master)
    params = jnp.zeros((BLOCKS, BLOCK), jnp.bfloat16).at[order].set(new_master.astype(jnp.bfloat16))
    return (new_master, new_first, new_second, params)
```

```python
import math

import jax
import jax.numpy as jnp
import numpy as np
from jax import lax
from jax.sharding import Mesh, PartitionSpec as P

beta_one = 0.9
beta_two = 0.95
first_fix = 1.0 - math.exp(100.0 * math.log(0.9))
second_fix = 1.0 - math.exp(100.0 * math.log(0.95))
learn_rate = 0.25
weight_decay = 0.1
epsilon = 1e-08

AXES = ("y_lo", "z", "core", "y_hi", "x")
SIZES = (4, 12, 2, 2, 4)


def hadamard_table(length, dtype):
    index = jnp.arange(length, dtype=jnp.int32)
    both = index[:, None] & index[None, :]
    parity = jnp.zeros((length, length), jnp.int32)
    for bit in range(length.bit_length() - 1):
        parity = parity + (jnp.right_shift(both, bit) & 1)
    parity = parity & 1
    return (1 - 2 * parity).astype(dtype)


def on_device(grads, sign_rows, sign_cols, block_order, master, first_moment, second_moment):
    held_grad = grads[0]
    block_len = held_grad.shape[1]
    inv_root = 1.0 / math.sqrt(block_len)
    lane_bf16 = hadamard_table(128, jnp.bfloat16)
    lane_float = hadamard_table(128, jnp.float32)
    sub_float = hadamard_table(16, jnp.float32)

    order_cm = block_order.reshape(48, 2, 2).transpose(1, 0, 2).reshape(192)
    pick = (order_cm[:, None] == jnp.arange(192, dtype=jnp.int32)[None, :]).astype(jnp.bfloat16)
    picked = jnp.dot(pick, held_grad, preferred_element_type=jnp.float32).astype(jnp.bfloat16)
    both_signs = jnp.concatenate([2 * sign_rows - 1, 2 * sign_cols - 1], axis=1).astype(jnp.bfloat16)
    signs = jnp.dot(pick, both_signs, preferred_element_type=jnp.float32).astype(jnp.bfloat16)
    signed = picked.reshape(192, 16, 128) * signs[:, :16, None] * signs[:, None, 16:]
    mixed = jnp.einsum("rac,cd->rad", signed, lane_bf16, preferred_element_type=jnp.float32)
    mixed = jnp.einsum("ba,rad->rbd", sub_float, mixed, precision=lax.Precision.HIGHEST)
    rotated = (mixed * inv_root).astype(jnp.bfloat16)
    sent = rotated.reshape(2, 96, 4, 4, 128).transpose(0, 2, 1, 3, 4).reshape(8, 384, 128)
    got = lax.all_to_all(sent, ("core", "x"), 0, 0, tiled=True)
    part = jnp.sum(got.astype(jnp.float32), axis=0).astype(jnp.bfloat16)
    sent = jnp.broadcast_to(part.reshape(48, 1, 8, 128), (48, 2, 8, 128)).reshape(96, 8, 128)
    got = lax.all_to_all(sent, ("y_lo", "z", "y_hi"), 0, 0, tiled=True)
    quarter = jnp.sum(got.astype(jnp.float32), axis=0)
    sent = jnp.broadcast_to(quarter[None], (4, 8, 128))
    got = lax.all_to_all(sent, "x", 0, 0, tiled=True)
    gradient = got.reshape(4, 2, 4, 128).transpose(1, 0, 2, 3).reshape(2, 16, 128)

    owner = (lax.axis_index("y_lo") * 12 + lax.axis_index("z")) * 2 + lax.axis_index("core")
    owned_blocks = lax.dynamic_slice_in_dim(block_order, owner * 2, 2)
    owned_signs = (
        (2 * jnp.take(sign_rows, owned_blocks, axis=0) - 1)[:, :, None]
        * (2 * jnp.take(sign_cols, owned_blocks, axis=0) - 1)[:, None, :]
    ).astype(jnp.float32)
    first_old = first_moment.reshape(2, 16, 128)
    second_old = second_moment.reshape(2, 16, 128)
    new_first = beta_one * first_old + (1.0 - beta_one) * gradient
    new_second = beta_two * second_old + (1.0 - beta_two) * gradient * gradient
    update = new_first / first_fix / (jnp.sqrt(new_second / second_fix) + epsilon)
    restored = jnp.einsum("ba,rad->rbd", sub_float, update, precision=lax.Precision.HIGHEST)
    restored = jnp.einsum("rbc,cd->rbd", restored, lane_float, precision=lax.Precision.HIGHEST)
    restored = (restored * inv_root * owned_signs).reshape(2, block_len)
    new_master = master - learn_rate * (restored + weight_decay * master)

    held = new_master.astype(jnp.bfloat16).reshape(2, 4, 4, 128)
    mine = lax.dynamic_slice_in_dim(held, lax.axis_index("x"), 1, axis=1).reshape(1, 8, 128)
    got = lax.all_to_all(jnp.broadcast_to(mine, (48, 8, 128)), ("y_lo", "z"), 0, 0, tiled=True)
    sent = jnp.broadcast_to(got.reshape(1, 384, 128), (4, 384, 128))
    got = lax.all_to_all(sent, "x", 0, 0, tiled=True)
    got = lax.all_gather(got.reshape(4 * 384, 128), "core", axis=0, tiled=True)
    by_slot = got.reshape(2, 4, 96, 4, 128).transpose(0, 2, 1, 3, 4).reshape(192, block_len)
    place = (jnp.arange(192, dtype=jnp.int32)[:, None] == order_cm[None, :]).astype(jnp.bfloat16)
    params = jnp.dot(place, by_slot, preferred_element_type=jnp.float32).astype(jnp.bfloat16)
    return (
        new_master,
        new_first.reshape(2, block_len),
        new_second.reshape(2, block_len),
        params,
    )


def solution(mesh):
    fine = Mesh(np.asarray(mesh.devices).reshape(SIZES), AXES)
    group = ("y_lo", "z", "core")
    placed = (
        P(AXES, None, None),
        P(),
        P(),
        P(),
        P(group, None),
        P(group, None),
        P(group, None),
    )
    return jax.shard_map(
        on_device,
        mesh=fine,
        in_specs=placed,
        out_specs=(P(group, None), P(group, None), P(group, None), P()),
        check_vma=False,
    )
```

```python
import math

import jax
import jax.numpy as jnp
import numpy as np
from jax import lax
from jax.sharding import Mesh, PartitionSpec as P

beta_one = 0.9
beta_two = 0.95
first_fix = 1.0 - math.exp(100.0 * math.log(0.9))
second_fix = 1.0 - math.exp(100.0 * math.log(0.95))
learn_rate = 0.25
weight_decay = 0.1
epsilon = 1e-08

AXES = ("y_lo", "z", "core", "y_hi", "x")
SIZES = (4, 12, 2, 2, 4)


def hadamard_table(length, dtype):
    index = jnp.arange(length, dtype=jnp.int32)
    both = index[:, None] & index[None, :]
    parity = jnp.zeros((length, length), jnp.int32)
    for bit in range(length.bit_length() - 1):
        parity = parity + (jnp.right_shift(both, bit) & 1)
    parity = parity & 1
    return (1 - 2 * parity).astype(dtype)


def on_device(grads, sign_rows, sign_cols, block_order, master, first_moment, second_moment):
    held_grad = grads[0]
    block_len = held_grad.shape[1]
    inv_root = 1.0 / math.sqrt(block_len)
    lane_bf16 = hadamard_table(128, jnp.bfloat16)
    lane_float = hadamard_table(128, jnp.float32)
    sub_float = hadamard_table(16, jnp.float32)

    core = lax.axis_index("core")
    order_table = block_order.reshape(4, 12, 2, 2).transpose(2, 1, 0, 3).reshape(2, 96)
    order_sent = jnp.where(core == 0, order_table[::-1], order_table).reshape(192)
    pick = (order_sent[:, None] == jnp.arange(192, dtype=jnp.int32)[None, :]).astype(jnp.bfloat16)
    picked = jnp.dot(pick, held_grad, preferred_element_type=jnp.float32).astype(jnp.bfloat16)
    both_signs = jnp.concatenate([2 * sign_rows - 1, 2 * sign_cols - 1], axis=1).astype(jnp.bfloat16)
    signs = jnp.dot(pick, both_signs, preferred_element_type=jnp.float32).astype(jnp.bfloat16)
    signed = picked.reshape(192, 16, 128) * signs[:, :16, None] * signs[:, None, 16:]
    mixed = jnp.einsum("rac,cd->rad", signed, lane_bf16, preferred_element_type=jnp.float32)
    mixed = jnp.einsum("ba,rad->rbd", sub_float, mixed, precision=lax.Precision.HIGHEST)
    rotated = (mixed * inv_root).astype(jnp.bfloat16)
    halves = rotated.reshape(2, 96, 4, 4, 128).transpose(0, 2, 1, 3, 4).reshape(2, 1536, 128)
    got = lax.all_gather(halves[0], "core", axis=0, tiled=True).reshape(2, 1536, 128)
    other = lax.dynamic_index_in_dim(got, 1 - core, 0, keepdims=False)
    part = (halves[1].astype(jnp.float32) + other.astype(jnp.float32)).astype(jnp.bfloat16)
    got = lax.all_to_all(part.reshape(4, 384, 128), "x", 0, 0, tiled=True)
    part = jnp.sum(got.astype(jnp.float32), axis=0).astype(jnp.bfloat16)
    got = lax.all_to_all(part.reshape(12, 32, 128), "z", 0, 0, tiled=True)
    part = jnp.sum(got.astype(jnp.float32), axis=0)
    sent = jnp.broadcast_to(part.reshape(4, 1, 8, 128), (4, 8, 8, 128)).reshape(32, 8, 128)
    got = lax.all_to_all(sent, ("y_lo", "y_hi", "x"), 0, 0, tiled=True)
    quarters = jnp.sum(got.reshape(8, 4, 8, 128), axis=0)
    gradient = quarters.reshape(4, 2, 4, 128).transpose(1, 0, 2, 3).reshape(2, 16, 128)

    owner = (lax.axis_index("y_lo") * 12 + lax.axis_index("z")) * 2 + lax.axis_index("core")
    owned_blocks = lax.dynamic_slice_in_dim(block_order, owner * 2, 2)
    owned_signs = (
        (2 * jnp.take(sign_rows, owned_blocks, axis=0) - 1)[:, :, None]
        * (2 * jnp.take(sign_cols, owned_blocks, axis=0) - 1)[:, None, :]
    ).astype(jnp.float32)
    first_old = first_moment.reshape(2, 16, 128)
    second_old = second_moment.reshape(2, 16, 128)
    new_first = beta_one * first_old + (1.0 - beta_one) * gradient
    new_second = beta_two * second_old + (1.0 - beta_two) * gradient * gradient
    update = new_first / first_fix / (jnp.sqrt(new_second / second_fix) + epsilon)
    restored = jnp.einsum("ba,rad->rbd", sub_float, update, precision=lax.Precision.HIGHEST)
    restored = jnp.einsum("rbc,cd->rbd", restored, lane_float, precision=lax.Precision.HIGHEST)
    restored = (restored * inv_root * owned_signs).reshape(2, block_len)
    new_master = master - learn_rate * (restored + weight_decay * master)

    held = new_master.astype(jnp.bfloat16).reshape(2, 4, 4, 128)
    mine = lax.dynamic_slice_in_dim(held, lax.axis_index("x"), 1, axis=1).reshape(1, 8, 128)
    got = lax.all_to_all(jnp.broadcast_to(mine, (48, 8, 128)), ("y_lo", "z"), 0, 0, tiled=True)
    sent = jnp.broadcast_to(got.reshape(1, 384, 128), (4, 384, 128))
    got = lax.all_to_all(sent, "x", 0, 0, tiled=True)
    got = lax.all_gather(got.reshape(4 * 384, 128), "core", axis=0, tiled=True)
    by_slot = got.reshape(2, 4, 96, 4, 128).transpose(0, 2, 1, 3, 4).reshape(192, block_len)
    order_got = block_order.reshape(48, 2, 2).transpose(1, 0, 2).reshape(192)
    place = (jnp.arange(192, dtype=jnp.int32)[:, None] == order_got[None, :]).astype(jnp.bfloat16)
    params = jnp.dot(place, by_slot, preferred_element_type=jnp.float32).astype(jnp.bfloat16)
    return (
        new_master,
        new_first.reshape(2, block_len),
        new_second.reshape(2, block_len),
        params,
    )


def solution(mesh):
    fine = Mesh(np.asarray(mesh.devices).reshape(SIZES), AXES)
    group = ("y_lo", "z", "core")
    placed = (
        P(AXES, None, None),
        P(),
        P(),
        P(),
        P(group, None),
        P(group, None),
        P(group, None),
    )
    return jax.shard_map(
        on_device,
        mesh=fine,
        in_specs=placed,
        out_specs=(P(group, None), P(group, None), P(group, None), P()),
        check_vma=False,
    )
```

```python
import math

import jax
import jax.numpy as jnp
import numpy as np
from jax import lax
from jax.experimental import pallas as pl
from jax.experimental.pallas import tpu as pltpu
from jax.sharding import Mesh, PartitionSpec as P

beta_one = 0.9
beta_two = 0.95
first_fix = 1.0 - math.exp(100.0 * math.log(0.9))
second_fix = 1.0 - math.exp(100.0 * math.log(0.95))
learn_rate = 0.25
weight_decay = 0.1
epsilon = 1e-08

AXES = ("y_lo", "z", "core", "y_hi", "x")
SIZES = (4, 12, 2, 2, 4)
BLOCKS = 192
BLOCK = 2048
LANE = 128
INV_ROOT = 1.0 / math.sqrt(BLOCK)
F32 = jnp.float32
BF16 = jnp.bfloat16


def iota(shape, axis):
    return lax.broadcasted_iota(jnp.int32, shape, axis)


def parity_sign(both, bits):
    for shift in bits:
        both = both ^ jnp.right_shift(both, shift)
    return (1 - 2 * (both & 1)).astype(F32)


def rotate_kernel(order_ref, rows_ref, cols_ref, grad_ref, out_ref):
    core = lax.axis_index("core")
    row = iota((BLOCKS, BLOCKS), 0)
    lane = iota((BLOCKS, BLOCKS), 1)
    half = (row >= 96).astype(jnp.int32)
    place = row - 96 * half
    y_lo = jnp.right_shift(place, 1) & 3
    z = jnp.right_shift(place, 3)
    owner = jnp.where(half == 1, core, 1 - core)
    slot = ((y_lo * 12 + z) * 2 + owner) * 2 + (place & 1)
    order = order_ref[...].astype(F32)
    block = jnp.sum(jnp.where(slot == lane, order, 0.0), axis=1, keepdims=True)
    pick = jnp.where(block == lane.astype(F32), 1.0, 0.0).astype(BF16)
    row_bits = (2 * rows_ref[...] - 1).astype(F32).astype(BF16)
    col_bits = (2 * cols_ref[...] - 1).astype(F32).astype(BF16)
    row_signs = lax.dot_general(pick, row_bits, (((1,), (1,)), ((), ())), preferred_element_type=F32)
    col_signs = jnp.dot(pick, col_bits, preferred_element_type=F32)
    table = parity_sign(iota((LANE, LANE), 0) & iota((LANE, LANE), 1), (4, 2, 1)).astype(BF16)
    mixed = []
    for a in range(16):
        picked = jnp.dot(pick, grad_ref[:, a * LANE : (a + 1) * LANE], preferred_element_type=F32)
        signed = (picked * col_signs * row_signs[:, a : a + 1]).astype(BF16)
        mixed.append(jnp.dot(signed, table, preferred_element_type=F32))
    span = 1
    while span < 16:
        for a in range(16):
            if not a & span:
                low, high = mixed[a], mixed[a + span]
                mixed[a], mixed[a + span] = low + high, low - high
        span *= 2
    for a in range(16):
        rotated = (mixed[a] * INV_ROOT).astype(BF16)
        quarter, column = a // 4, (a % 4) * LANE
        out_ref[0, quarter, :, column : column + LANE] = rotated[:96]
        out_ref[1, quarter, :, column : column + LANE] = rotated[96:]


def owned_signs_kernel(owned_ref, rows_ref, cols_ref, out_ref):
    row = iota((32, BLOCKS), 0)
    lane = iota((32, BLOCKS), 1)
    wanted = jnp.where((row & 1) == 0, owned_ref[0], owned_ref[1])
    pick = jnp.where(lane == wanted, 1.0, 0.0)
    spread = jnp.where(iota((32, 16), 1) == jnp.right_shift(iota((32, 16), 0), 1), 1.0, 0.0).astype(BF16)
    row_bits = (2 * rows_ref[...] - 1).astype(F32).astype(BF16)
    col_bits = (2 * cols_ref[...] - 1).astype(F32).astype(BF16)
    wide = jnp.dot(spread, row_bits, preferred_element_type=F32)
    row_signs = jnp.sum(wide * pick, axis=1, keepdims=True)
    col_signs = jnp.dot(pick.astype(BF16), col_bits, preferred_element_type=F32)
    out_ref[...] = row_signs * col_signs


def adam_kernel(got_ref, signs_ref, master_ref, first_ref, second_ref, new_master_ref, new_first_ref, new_second_ref, sent_ref, held_ref):
    total = got_ref[0:4]
    for y in range(1, 8):
        total = total + got_ref[4 * y : 4 * y + 4]
    gradient = total.reshape(32, LANE)
    new_first = beta_one * first_ref[...] + (1.0 - beta_one) * gradient
    new_second = beta_two * second_ref[...] + (1.0 - beta_two) * gradient * gradient
    new_first_ref[...] = new_first
    new_second_ref[...] = new_second
    update = new_first / first_fix / (jnp.sqrt(new_second / second_fix) + epsilon)
    row, col = iota((32, 32), 0), iota((32, 32), 1)
    same = ((row ^ col) & 1) == 0
    sub = jnp.where(same, parity_sign(jnp.right_shift(row & col, 1), (2, 1)), 0.0)
    table = parity_sign(iota((LANE, LANE), 0) & iota((LANE, LANE), 1), (4, 2, 1))
    restored = jnp.dot(sub, update, precision=lax.Precision.HIGHEST, preferred_element_type=F32)
    restored = jnp.dot(restored, table, precision=lax.Precision.HIGHEST, preferred_element_type=F32)
    restored = restored * INV_ROOT * signs_ref[...]
    master = master_ref[...]
    new_master = master - learn_rate * (restored + weight_decay * master)
    new_master_ref[...] = new_master
    held_ref[...] = new_master
    start = pl.multiple_of(lax.axis_index("x") * 8, 8)
    mine = held_ref[pl.ds(start, 8), :].astype(BF16)
    for member in range(48):
        sent_ref[member] = mine


def place_kernel(order_ref, out_ref):
    col = iota((BLOCKS, 768), 1)
    core = (col >= 384).astype(jnp.int32)
    rest = col - 384 * core
    slot = (jnp.right_shift(rest, 3) * 2 + core) * 2 + (rest & 1)
    spread = jnp.where(iota((BLOCKS, 768), 0) == slot, 1.0, 0.0).astype(BF16)
    order = jnp.broadcast_to(order_ref[...].astype(F32), (8, BLOCKS)).astype(BF16)
    block = jnp.dot(order, spread, preferred_element_type=F32)[0:1]
    match = iota((BLOCKS, 768), 0).astype(F32) == block
    part = jnp.right_shift(rest, 1) & 3
    for a in range(4):
        out_ref[a * BLOCKS : (a + 1) * BLOCKS, :] = jnp.where(match & (part == a), 1.0, 0.0).astype(BF16)


def params_kernel(place_ref, got_ref, out_ref):
    for x in range(4):
        rows = jnp.concatenate([got_ref[0, x], got_ref[1, x]], axis=0)
        placed = jnp.dot(place_ref[...], rows, preferred_element_type=F32).astype(BF16)
        for a in range(4):
            column = (4 * x + a) * LANE
            out_ref[:, column : column + LANE] = placed[a * BLOCKS : (a + 1) * BLOCKS]


VMEM = pl.BlockSpec(memory_space=pltpu.VMEM)
SMEM = pl.BlockSpec(memory_space=pltpu.SMEM)
ROOM = pltpu.CompilerParams(vmem_limit_bytes=32 * 1024 * 1024)


def on_device(grads, sign_rows, sign_cols, block_order, master, first_moment, second_moment):
    core = lax.axis_index("core")
    order_row = block_order.reshape(1, BLOCKS)
    rows_t = sign_rows.T

    halves = pl.pallas_call(
        rotate_kernel,
        out_shape=jax.ShapeDtypeStruct((2, 4, 96, 512), BF16),
        in_specs=[VMEM] * 4,
        out_specs=VMEM,
        compiler_params=ROOM,
        name="rotate",
    )(order_row, rows_t, sign_cols, grads[0])
    got = lax.all_gather(halves[0].reshape(384, 512), "core", axis=0, tiled=True).reshape(2, 4, 96, 512)
    other = lax.dynamic_index_in_dim(got, 1 - core, 0, keepdims=False)
    part = (halves[1].astype(F32) + other.astype(F32)).astype(BF16)
    got = lax.all_to_all(part, "x", 0, 0, tiled=True)
    part = jnp.sum(got.astype(F32), axis=0).astype(BF16)
    got = lax.all_to_all(part.reshape(12, 8, 512), "z", 0, 0, tiled=True)
    part = jnp.sum(got.astype(F32), axis=0)
    part = part.reshape(4, 2, 4, LANE).transpose(0, 2, 1, 3).reshape(4, 1, 8, LANE)
    sent = jnp.broadcast_to(part, (4, 8, 8, LANE)).reshape(32, 8, LANE)
    got = lax.all_to_all(sent, ("y_lo", "y_hi", "x"), 0, 0, tiled=True)

    owner = (lax.axis_index("y_lo") * 12 + lax.axis_index("z")) * 2 + core
    owned = lax.dynamic_slice_in_dim(block_order, owner * 2, 2)
    signs = pl.pallas_call(
        owned_signs_kernel,
        out_shape=jax.ShapeDtypeStruct((32, LANE), F32),
        in_specs=[SMEM, VMEM, VMEM],
        out_specs=VMEM,
        compiler_params=ROOM,
        cost_estimate=pl.CostEstimate(flops=2000000, bytes_accessed=200000, transcendentals=0),
        name="owned_signs",
    )(owned, rows_t, sign_cols)

    def by_row(value):
        return value.reshape(2, 16, LANE).transpose(1, 0, 2).reshape(32, LANE)

    def by_slot(value):
        return value.reshape(16, 2, LANE).transpose(1, 0, 2).reshape(2, BLOCK)

    state = jax.ShapeDtypeStruct((32, LANE), F32)
    new_master, new_first, new_second, sent = pl.pallas_call(
        adam_kernel,
        out_shape=(state, state, state, jax.ShapeDtypeStruct((48, 8, LANE), BF16)),
        in_specs=[VMEM] * 5,
        out_specs=(VMEM,) * 4,
        scratch_shapes=[pltpu.VMEM((32, LANE), F32)],
        compiler_params=ROOM,
        name="adam",
    )(got, signs, by_row(master), by_row(first_moment), by_row(second_moment))

    got = lax.all_to_all(sent, ("y_lo", "z"), 0, 0, tiled=True)
    sent = jnp.broadcast_to(got.reshape(1, 384, LANE), (4, 384, LANE))
    got = lax.all_to_all(sent, "x", 0, 0, tiled=True)
    got = lax.all_gather(got.reshape(1536, LANE), "core", axis=0, tiled=True).reshape(2, 4, 384, LANE)

    place = pl.pallas_call(
        place_kernel,
        out_shape=jax.ShapeDtypeStruct((768, 768), BF16),
        in_specs=[VMEM],
        out_specs=VMEM,
        compiler_params=ROOM,
        cost_estimate=pl.CostEstimate(flops=4000000, bytes_accessed=1200000, transcendentals=0),
        name="place",
    )(order_row)
    params = pl.pallas_call(
        params_kernel,
        out_shape=jax.ShapeDtypeStruct((BLOCKS, BLOCK), BF16),
        in_specs=[VMEM] * 2,
        out_specs=VMEM,
        compiler_params=ROOM,
        name="params",
    )(place, got)
    return by_slot(new_master), by_slot(new_first), by_slot(new_second), params


def solution(mesh):
    fine = Mesh(np.asarray(mesh.devices).reshape(SIZES), AXES)
    group = ("y_lo", "z", "core")
    placed = (
        P(AXES, None, None),
        P(),
        P(),
        P(),
        P(group, None),
        P(group, None),
        P(group, None),
    )
    return jax.shard_map(
        on_device,
        mesh=fine,
        in_specs=placed,
        out_specs=(P(group, None), P(group, None), P(group, None), P()),
        check_vma=False,
    )
```

```python
import math

import jax
import jax.numpy as jnp
import numpy as np
from jax import lax
from jax.experimental import pallas as pl
from jax.experimental.pallas import tpu as pltpu
from jax.sharding import Mesh, PartitionSpec as P

beta_one = 0.9
beta_two = 0.95
first_fix = 1.0 - math.exp(100.0 * math.log(0.9))
second_fix = 1.0 - math.exp(100.0 * math.log(0.95))
learn_rate = 0.25
weight_decay = 0.1
epsilon = 1e-08

AXES = ("y_lo", "z", "core", "y_hi", "x")
SIZES = (4, 12, 2, 2, 4)
BLOCKS = 192
BLOCK = 2048
LANE = 128
INV_ROOT = 1.0 / math.sqrt(BLOCK)
F32 = jnp.float32
BF16 = jnp.bfloat16


def iota(shape, axis):
    return lax.broadcasted_iota(jnp.int32, shape, axis)


def parity_sign(both, bits):
    for shift in bits:
        both = both ^ jnp.right_shift(both, shift)
    return (1 - 2 * (both & 1)).astype(F32)


def rotate_kernel(order_hbm, rows_hbm, cols_hbm, grad_hbm, out_ref, order_ref, rows_ref, cols_ref, grad_ref, mixed_ref, sems):
    small = [
        pltpu.make_async_copy(order_hbm, order_ref, sems.at[0]),
        pltpu.make_async_copy(rows_hbm, rows_ref, sems.at[1]),
        pltpu.make_async_copy(cols_hbm, cols_ref, sems.at[2]),
    ]
    large = [
        pltpu.make_async_copy(
            grad_hbm.at[:, k * 512 : (k + 1) * 512], grad_ref.at[:, k * 512 : (k + 1) * 512], sems.at[3 + k]
        )
        for k in range(4)
    ]
    for copy in small + large:
        copy.start()
    core = lax.axis_index("core")
    row = iota((BLOCKS, BLOCKS), 0)
    lane = iota((BLOCKS, BLOCKS), 1)
    half = (row >= 96).astype(jnp.int32)
    place = row - 96 * half
    y_lo = jnp.right_shift(place, 1) & 3
    z = jnp.right_shift(place, 3)
    owner = jnp.where(half == 1, core, 1 - core)
    slot = ((y_lo * 12 + z) * 2 + owner) * 2 + (place & 1)
    table = parity_sign(iota((256, 256), 0) & iota((256, 256), 1), (4, 2, 1)).astype(BF16)
    for copy in small:
        copy.wait()
    order = order_ref[...].astype(F32)
    block = jnp.sum(jnp.where(slot == lane, order, 0.0), axis=1, keepdims=True)
    pick = jnp.where(block == lane.astype(F32), 1.0, 0.0).astype(BF16)
    row_bits = (2 * rows_ref[...] - 1).astype(F32).astype(BF16)
    col_bits = (2 * cols_ref[...] - 1).astype(F32).astype(BF16)
    row_signs = lax.dot_general(pick, row_bits, (((1,), (1,)), ((), ())), preferred_element_type=F32)
    col_signs = jnp.dot(pick, col_bits, preferred_element_type=F32)
    for k in range(8):
        if k % 2 == 0:
            large[k // 2].wait()
        picked = jnp.dot(pick, grad_ref[:, k * 256 : (k + 1) * 256], preferred_element_type=F32)
        signed = jnp.concatenate(
            [
                picked[:, :LANE] * col_signs * row_signs[:, 2 * k : 2 * k + 1],
                picked[:, LANE:] * col_signs * row_signs[:, 2 * k + 1 : 2 * k + 2],
            ],
            axis=1,
        ).astype(BF16)
        mixed_ref[k] = jnp.dot(signed, table, preferred_element_type=F32)
    for start in range(0, BLOCKS, 16):
        mixed = [mixed_ref[k, start : start + 16] for k in range(8)]
        for span in (1, 2, 4):
            for k in range(8):
                if not k & span:
                    low, high = mixed[k], mixed[k + span]
                    mixed[k], mixed[k + span] = low + high, low - high
        for k in range(8):
            rotated = (mixed[k] * INV_ROOT).astype(BF16)
            out_ref[start // 96, k // 2, start % 96 : start % 96 + 16, (k % 2) * 256 : (k % 2) * 256 + 256] = rotated


def owner_sum_kernel(got_ref, out_ref):
    total = got_ref[0].astype(F32)
    for z in range(1, 12):
        total = total + got_ref[z].astype(F32)
    for y_lo in range(4):
        piece = jnp.concatenate(
            [total[2 * y_lo : 2 * y_lo + 2, a * LANE : (a + 1) * LANE] for a in range(4)], axis=0
        )
        for member in range(8):
            out_ref[8 * y_lo + member] = piece


def owned_signs_kernel(owned_ref, rows_ref, cols_ref, out_ref):
    row = iota((32, BLOCKS), 0)
    lane = iota((32, BLOCKS), 1)
    wanted = jnp.where((row & 1) == 0, owned_ref[0], owned_ref[1])
    pick = jnp.where(lane == wanted, 1.0, 0.0)
    spread = jnp.where(iota((32, 16), 1) == jnp.right_shift(iota((32, 16), 0), 1), 1.0, 0.0).astype(BF16)
    row_bits = (2 * rows_ref[...] - 1).astype(F32).astype(BF16)
    col_bits = (2 * cols_ref[...] - 1).astype(F32).astype(BF16)
    wide = jnp.dot(spread, row_bits, preferred_element_type=F32)
    row_signs = jnp.sum(wide * pick, axis=1, keepdims=True)
    col_signs = jnp.dot(pick.astype(BF16), col_bits, preferred_element_type=F32)
    out_ref[...] = row_signs * col_signs


def adam_kernel(got_ref, signs_ref, master_ref, first_ref, second_ref, new_master_ref, new_first_ref, new_second_ref, sent_ref, held_ref):
    total = got_ref[0:4]
    for y in range(1, 8):
        total = total + got_ref[4 * y : 4 * y + 4]
    gradient = total.reshape(32, LANE)
    new_first = beta_one * first_ref[...] + (1.0 - beta_one) * gradient
    new_second = beta_two * second_ref[...] + (1.0 - beta_two) * gradient * gradient
    new_first_ref[...] = new_first
    new_second_ref[...] = new_second
    update = new_first / first_fix / (jnp.sqrt(new_second / second_fix) + epsilon)
    row, col = iota((32, 32), 0), iota((32, 32), 1)
    same = ((row ^ col) & 1) == 0
    sub = jnp.where(same, parity_sign(jnp.right_shift(row & col, 1), (2, 1)), 0.0)
    table = parity_sign(iota((LANE, LANE), 0) & iota((LANE, LANE), 1), (4, 2, 1))
    restored = jnp.dot(sub, update, precision=lax.Precision.HIGHEST, preferred_element_type=F32)
    restored = jnp.dot(restored, table, precision=lax.Precision.HIGHEST, preferred_element_type=F32)
    restored = restored * INV_ROOT * signs_ref[...]
    master = master_ref[...]
    new_master = master - learn_rate * (restored + weight_decay * master)
    new_master_ref[...] = new_master
    held_ref[...] = new_master
    start = pl.multiple_of(lax.axis_index("x") * 8, 8)
    mine = held_ref[pl.ds(start, 8), :].astype(BF16)
    for member in range(48):
        sent_ref[member] = mine


def place_kernel(order_ref, out_ref):
    col = iota((BLOCKS, BLOCKS), 1)
    core = (col >= 96).astype(jnp.int32)
    rest = col - 96 * core
    j = (rest >= 48).astype(jnp.int32)
    slot = ((rest - 48 * j) * 2 + core) * 2 + j
    spread = jnp.where(iota((BLOCKS, BLOCKS), 0) == slot, 1.0, 0.0).astype(BF16)
    order = jnp.broadcast_to(order_ref[...].astype(F32), (8, BLOCKS)).astype(BF16)
    block = jnp.dot(order, spread, preferred_element_type=F32)[0:1]
    out_ref[...] = jnp.where(iota((BLOCKS, BLOCKS), 0).astype(F32) == block, 1.0, 0.0).astype(BF16)


def repeat_kernel(got_ref, out_ref, wide_ref):
    wide_ref[...] = got_ref[...].astype(F32)
    for a in range(4):
        rows = jnp.concatenate(
            [wide_ref[pl.ds(2 * a + j, 48, stride=8), :] for j in range(2)], axis=0
        ).astype(BF16)
        for x in range(4):
            out_ref[x, :, a * LANE : (a + 1) * LANE] = rows


def params_kernel(place_ref, got_ref, out_hbm, out_ref, sems):
    copies = []
    for x in range(4):
        rows = jnp.concatenate([got_ref[0, x], got_ref[1, x]], axis=0)
        column = x * 512
        placed = jnp.dot(place_ref[...], rows, preferred_element_type=F32)
        out_ref[:, column : column + 512] = placed.astype(BF16)
        copy = pltpu.make_async_copy(
            out_ref.at[:, column : column + 512], out_hbm.at[:, column : column + 512], sems.at[x]
        )
        copy.start()
        copies.append(copy)
    for copy in copies:
        copy.wait()


VMEM = pl.BlockSpec(memory_space=pltpu.VMEM)
SMEM = pl.BlockSpec(memory_space=pltpu.SMEM)
HBM = pl.BlockSpec(memory_space=pltpu.HBM)
ROOM = pltpu.CompilerParams(vmem_limit_bytes=32 * 1024 * 1024)


def on_device(grads, sign_rows, sign_cols, block_order, master, first_moment, second_moment):
    core = lax.axis_index("core")
    order_row = block_order.reshape(1, BLOCKS)
    rows_t = sign_rows.T

    halves = pl.pallas_call(
        rotate_kernel,
        out_shape=jax.ShapeDtypeStruct((2, 4, 96, 512), BF16),
        in_specs=[HBM] * 4,
        out_specs=VMEM,
        scratch_shapes=[
            pltpu.VMEM((1, BLOCKS), jnp.int32),
            pltpu.VMEM((16, BLOCKS), jnp.int32),
            pltpu.VMEM((BLOCKS, LANE), jnp.int32),
            pltpu.VMEM((BLOCKS, BLOCK), BF16),
            pltpu.VMEM((8, BLOCKS, 256), F32),
            pltpu.SemaphoreType.DMA((7,)),
        ],
        compiler_params=ROOM,
        name="rotate",
    )(order_row, rows_t, sign_cols, grads[0])
    got = lax.all_gather(halves[0].reshape(384, 512), "core", axis=0, tiled=True).reshape(2, 4, 96, 512)
    other = lax.dynamic_index_in_dim(got, 1 - core, 0, keepdims=False)
    part = (halves[1].astype(F32) + other.astype(F32)).astype(BF16)
    got = lax.all_to_all(part, "x", 0, 0, tiled=True)
    part = jnp.sum(got.astype(F32), axis=0).astype(BF16)
    got = lax.all_to_all(part.reshape(12, 8, 512), "z", 0, 0, tiled=True)
    sent = pl.pallas_call(
        owner_sum_kernel,
        out_shape=jax.ShapeDtypeStruct((32, 8, LANE), F32),
        in_specs=[VMEM],
        out_specs=VMEM,
        compiler_params=ROOM,
        name="owner_sum",
    )(got)
    got = lax.all_to_all(sent, ("y_lo", "y_hi", "x"), 0, 0, tiled=True)

    owner = (lax.axis_index("y_lo") * 12 + lax.axis_index("z")) * 2 + core
    owned = lax.dynamic_slice_in_dim(block_order, owner * 2, 2)
    signs = pl.pallas_call(
        owned_signs_kernel,
        out_shape=jax.ShapeDtypeStruct((32, LANE), F32),
        in_specs=[SMEM, VMEM, VMEM],
        out_specs=VMEM,
        compiler_params=ROOM,
        cost_estimate=pl.CostEstimate(flops=2000000, bytes_accessed=200000, transcendentals=0),
        name="owned_signs",
    )(owned, rows_t, sign_cols)

    def by_row(value):
        return value.reshape(2, 16, LANE).transpose(1, 0, 2).reshape(32, LANE)

    def by_slot(value):
        return value.reshape(16, 2, LANE).transpose(1, 0, 2).reshape(2, BLOCK)

    state = jax.ShapeDtypeStruct((32, LANE), F32)
    new_master, new_first, new_second, sent = pl.pallas_call(
        adam_kernel,
        out_shape=(state, state, state, jax.ShapeDtypeStruct((48, 8, LANE), BF16)),
        in_specs=[VMEM] * 5,
        out_specs=(VMEM,) * 4,
        scratch_shapes=[pltpu.VMEM((32, LANE), F32)],
        compiler_params=ROOM,
        name="adam",
    )(got, signs, by_row(master), by_row(first_moment), by_row(second_moment))

    got = lax.all_to_all(sent, ("y_lo", "z"), 0, 0, tiled=True)
    sent = pl.pallas_call(
        repeat_kernel,
        out_shape=jax.ShapeDtypeStruct((4, 96, 512), BF16),
        in_specs=[VMEM],
        out_specs=VMEM,
        scratch_shapes=[pltpu.VMEM((384, LANE), F32)],
        compiler_params=ROOM,
        name="repeat",
    )(got.reshape(384, LANE))
    got = lax.all_to_all(sent, "x", 0, 0, tiled=True)
    got = lax.all_gather(got.reshape(384, 512), "core", axis=0, tiled=True).reshape(2, 4, 96, 512)

    place = pl.pallas_call(
        place_kernel,
        out_shape=jax.ShapeDtypeStruct((BLOCKS, BLOCKS), BF16),
        in_specs=[VMEM],
        out_specs=VMEM,
        compiler_params=ROOM,
        cost_estimate=pl.CostEstimate(flops=4000000, bytes_accessed=1200000, transcendentals=0),
        name="place",
    )(order_row)
    params = pl.pallas_call(
        params_kernel,
        out_shape=jax.ShapeDtypeStruct((BLOCKS, BLOCK), BF16),
        in_specs=[VMEM] * 2,
        out_specs=HBM,
        scratch_shapes=[pltpu.VMEM((BLOCKS, BLOCK), BF16), pltpu.SemaphoreType.DMA((4,))],
        compiler_params=ROOM,
        name="params",
    )(place, got)
    return by_slot(new_master), by_slot(new_first), by_slot(new_second), params


def solution(mesh):
    fine = Mesh(np.asarray(mesh.devices).reshape(SIZES), AXES)
    group = ("y_lo", "z", "core")
    placed = (
        P(AXES, None, None),
        P(),
        P(),
        P(),
        P(group, None),
        P(group, None),
        P(group, None),
    )
    return jax.shard_map(
        on_device,
        mesh=fine,
        in_specs=placed,
        out_specs=(P(group, None), P(group, None), P(group, None), P()),
        check_vma=False,
    )
```

```python
import math

import jax
import jax.numpy as jnp
import numpy as np
from jax import lax
from jax.experimental import pallas as pl
from jax.experimental.pallas import tpu as pltpu
from jax.sharding import Mesh, PartitionSpec as P

beta_one = 0.9
beta_two = 0.95
first_fix = 1.0 - math.exp(100.0 * math.log(0.9))
second_fix = 1.0 - math.exp(100.0 * math.log(0.95))
learn_rate = 0.25
weight_decay = 0.1
epsilon = 1e-08

AXES = ("y_lo", "z", "core", "y_hi", "x")
SIZES = (4, 12, 2, 2, 4)
BLOCKS = 192
BLOCK = 2048
LANE = 128
INV_ROOT = 1.0 / math.sqrt(BLOCK)
F32 = jnp.float32
BF16 = jnp.bfloat16


def iota(shape, axis):
    return lax.broadcasted_iota(jnp.int32, shape, axis)


def parity_sign(both, bits):
    for shift in bits:
        both = both ^ jnp.right_shift(both, shift)
    return (1 - 2 * (both & 1)).astype(F32)


def rotate_kernel(order_hbm, rows_hbm, cols_hbm, grad_hbm, out_ref, order_ref, rows_ref, cols_ref, grad_ref, mixed_ref, sems):
    small = [
        pltpu.make_async_copy(order_hbm, order_ref, sems.at[0]),
        pltpu.make_async_copy(rows_hbm, rows_ref, sems.at[1]),
        pltpu.make_async_copy(cols_hbm, cols_ref, sems.at[2]),
    ]
    large = [
        pltpu.make_async_copy(
            grad_hbm.at[:, k * 512 : (k + 1) * 512], grad_ref.at[:, k * 512 : (k + 1) * 512], sems.at[3 + k]
        )
        for k in range(4)
    ]
    for copy in small + large:
        copy.start()
    core = lax.axis_index("core")
    row = iota((BLOCKS, BLOCKS), 0)
    lane = iota((BLOCKS, BLOCKS), 1)
    half = (row >= 96).astype(jnp.int32)
    place = row - 96 * half
    y_lo = jnp.right_shift(place, 1) & 3
    z = jnp.right_shift(place, 3)
    owner = jnp.where(half == 1, core, 1 - core)
    slot = ((y_lo * 12 + z) * 2 + owner) * 2 + (place & 1)
    table = parity_sign(iota((256, 256), 0) & iota((256, 256), 1), (4, 2, 1)).astype(BF16)
    for copy in small:
        copy.wait()
    order = order_ref[...].astype(F32)
    block = jnp.sum(jnp.where(slot == lane, order, 0.0), axis=1, keepdims=True)
    pick = jnp.where(block == lane.astype(F32), 1.0, 0.0).astype(BF16)
    row_bits = (2 * rows_ref[...] - 1).astype(F32).astype(BF16)
    col_bits = (2 * cols_ref[...] - 1).astype(F32).astype(BF16)
    row_signs = lax.dot_general(pick, row_bits, (((1,), (1,)), ((), ())), preferred_element_type=F32)
    col_signs = jnp.dot(pick, col_bits, preferred_element_type=F32)
    for k in range(8):
        if k % 2 == 0:
            large[k // 2].wait()
        picked = jnp.dot(pick, grad_ref[:, k * 256 : (k + 1) * 256], preferred_element_type=F32)
        signed = jnp.concatenate(
            [
                picked[:, :LANE] * col_signs * row_signs[:, 2 * k : 2 * k + 1],
                picked[:, LANE:] * col_signs * row_signs[:, 2 * k + 1 : 2 * k + 2],
            ],
            axis=1,
        ).astype(BF16)
        mixed_ref[k] = jnp.dot(signed, table, preferred_element_type=F32)
    for start in range(0, BLOCKS, 16):
        mixed = [mixed_ref[k, start : start + 16] for k in range(8)]
        for span in (1, 2, 4):
            for k in range(8):
                if not k & span:
                    low, high = mixed[k], mixed[k + span]
                    mixed[k], mixed[k + span] = low + high, low - high
        for k in range(8):
            rotated = (mixed[k] * INV_ROOT).astype(BF16)
            out_ref[start // 96, k // 2, start % 96 : start % 96 + 16, (k % 2) * 256 : (k % 2) * 256 + 256] = rotated


def owner_sum_kernel(got_ref, out_ref):
    total = got_ref[0].astype(F32)
    for z in range(1, 12):
        total = total + got_ref[z].astype(F32)
    for y_lo in range(4):
        piece = jnp.concatenate(
            [total[2 * y_lo : 2 * y_lo + 2, a * LANE : (a + 1) * LANE] for a in range(4)], axis=0
        )
        for member in range(8):
            out_ref[8 * y_lo + member] = piece


def owned_signs_kernel(owned_ref, rows_ref, cols_ref, out_ref):
    row = iota((32, BLOCKS), 0)
    lane = iota((32, BLOCKS), 1)
    wanted = jnp.where((row & 1) == 0, owned_ref[0], owned_ref[1])
    pick = jnp.where(lane == wanted, 1.0, 0.0)
    spread = jnp.where(iota((32, 16), 1) == jnp.right_shift(iota((32, 16), 0), 1), 1.0, 0.0).astype(BF16)
    row_bits = (2 * rows_ref[...] - 1).astype(F32).astype(BF16)
    col_bits = (2 * cols_ref[...] - 1).astype(F32).astype(BF16)
    wide = jnp.dot(spread, row_bits, preferred_element_type=F32)
    row_signs = jnp.sum(wide * pick, axis=1, keepdims=True)
    col_signs = jnp.dot(pick.astype(BF16), col_bits, preferred_element_type=F32)
    out_ref[...] = row_signs * col_signs


def adam_kernel(got_ref, signs_ref, master_ref, first_ref, second_ref, new_master_ref, new_first_ref, new_second_ref, sent_ref, held_ref):
    total = got_ref[0:4]
    for y in range(1, 8):
        total = total + got_ref[4 * y : 4 * y + 4]
    gradient = total.reshape(32, LANE)
    new_first = beta_one * first_ref[...] + (1.0 - beta_one) * gradient
    new_second = beta_two * second_ref[...] + (1.0 - beta_two) * gradient * gradient
    new_first_ref[...] = new_first
    new_second_ref[...] = new_second
    update = new_first / first_fix / (jnp.sqrt(new_second / second_fix) + epsilon)
    row, col = iota((32, 32), 0), iota((32, 32), 1)
    same = ((row ^ col) & 1) == 0
    sub = jnp.where(same, parity_sign(jnp.right_shift(row & col, 1), (2, 1)), 0.0)
    table = parity_sign(iota((LANE, LANE), 0) & iota((LANE, LANE), 1), (4, 2, 1))
    restored = jnp.dot(sub, update, precision=lax.Precision.HIGHEST, preferred_element_type=F32)
    restored = jnp.dot(restored, table, precision=lax.Precision.HIGHEST, preferred_element_type=F32)
    restored = restored * INV_ROOT * signs_ref[...]
    master = master_ref[...]
    new_master = master - learn_rate * (restored + weight_decay * master)
    new_master_ref[...] = new_master
    held_ref[...] = new_master
    start = pl.multiple_of(lax.axis_index("x") * 8, 8)
    mine = held_ref[pl.ds(start, 8), :].astype(BF16)
    for member in range(48):
        sent_ref[member] = mine


def place_kernel(order_ref, out_ref):
    col = iota((BLOCKS, BLOCKS), 1)
    core = (col >= 96).astype(jnp.int32)
    rest = col - 96 * core
    j = (rest >= 48).astype(jnp.int32)
    slot = ((rest - 48 * j) * 2 + core) * 2 + j
    spread = jnp.where(iota((BLOCKS, BLOCKS), 0) == slot, 1.0, 0.0).astype(BF16)
    order = jnp.broadcast_to(order_ref[...].astype(F32), (8, BLOCKS)).astype(BF16)
    block = jnp.dot(order, spread, preferred_element_type=F32)[0:1]
    out_ref[...] = jnp.where(iota((BLOCKS, BLOCKS), 0).astype(F32) == block, 1.0, 0.0).astype(BF16)


def repeat_kernel(got_ref, out_ref, wide_ref):
    wide_ref[...] = got_ref[...].astype(F32)
    for a in range(4):
        rows = jnp.concatenate(
            [wide_ref[pl.ds(2 * a + j, 48, stride=8), :] for j in range(2)], axis=0
        ).astype(BF16)
        for x in range(4):
            out_ref[x, :, a * LANE : (a + 1) * LANE] = rows


def params_kernel(place_ref, got_ref, out_hbm, out_ref, sems):
    copies = []
    for x in range(4):
        rows = jnp.concatenate([got_ref[0, x], got_ref[1, x]], axis=0)
        column = x * 512
        placed = jnp.dot(place_ref[...], rows, preferred_element_type=F32)
        out_ref[:, column : column + 512] = placed.astype(BF16)
        copy = pltpu.make_async_copy(
            out_ref.at[:, column : column + 512], out_hbm.at[:, column : column + 512], sems.at[x]
        )
        copy.start()
        copies.append(copy)
    for copy in copies:
        copy.wait()


VMEM = pl.BlockSpec(memory_space=pltpu.VMEM)
SMEM = pl.BlockSpec(memory_space=pltpu.SMEM)
HBM = pl.BlockSpec(memory_space=pltpu.HBM)
ROOM = pltpu.CompilerParams(vmem_limit_bytes=32 * 1024 * 1024)


def on_device(grads, sign_rows, sign_cols, block_order, master, first_moment, second_moment):
    core = lax.axis_index("core")
    order_row = block_order.reshape(1, BLOCKS)
    rows_t = sign_rows.T

    halves = pl.pallas_call(
        rotate_kernel,
        out_shape=jax.ShapeDtypeStruct((2, 4, 96, 512), BF16),
        in_specs=[HBM] * 4,
        out_specs=VMEM,
        scratch_shapes=[
            pltpu.VMEM((1, BLOCKS), jnp.int32),
            pltpu.VMEM((16, BLOCKS), jnp.int32),
            pltpu.VMEM((BLOCKS, LANE), jnp.int32),
            pltpu.VMEM((BLOCKS, BLOCK), BF16),
            pltpu.VMEM((8, BLOCKS, 256), F32),
            pltpu.SemaphoreType.DMA((7,)),
        ],
        compiler_params=ROOM,
        name="rotate",
    )(*(pltpu.with_memory_space_constraint(each, pltpu.HBM) for each in (order_row, rows_t, sign_cols, grads[0])))
    got = lax.all_gather(halves[0].reshape(384, 512), "core", axis=0, tiled=True).reshape(2, 4, 96, 512)
    other = lax.dynamic_index_in_dim(got, 1 - core, 0, keepdims=False)
    part = (halves[1].astype(F32) + other.astype(F32)).astype(BF16)
    got = lax.all_to_all(part, "x", 0, 0, tiled=True)
    part = jnp.sum(got.astype(F32), axis=0).astype(BF16)
    part, order_late, rows_late, cols_late = lax.optimization_barrier((part, block_order, rows_t, sign_cols))
    got = lax.all_to_all(part.reshape(12, 8, 512), "z", 0, 0, tiled=True)
    owner = (lax.axis_index("y_lo") * 12 + lax.axis_index("z")) * 2 + core
    owned = lax.dynamic_slice_in_dim(order_late, owner * 2, 2)
    signs = pl.pallas_call(
        owned_signs_kernel,
        out_shape=jax.ShapeDtypeStruct((32, LANE), F32),
        in_specs=[SMEM, VMEM, VMEM],
        out_specs=VMEM,
        compiler_params=ROOM,
        cost_estimate=pl.CostEstimate(flops=2000000, bytes_accessed=200000, transcendentals=0),
        name="owned_signs",
    )(owned, rows_late, cols_late)

    place = pl.pallas_call(
        place_kernel,
        out_shape=jax.ShapeDtypeStruct((BLOCKS, BLOCKS), BF16),
        in_specs=[VMEM],
        out_specs=VMEM,
        compiler_params=ROOM,
        cost_estimate=pl.CostEstimate(flops=4000000, bytes_accessed=1200000, transcendentals=0),
        name="place",
    )(order_late.reshape(1, BLOCKS))
    got, signs, place = lax.optimization_barrier((got, signs, place))
    sent = pl.pallas_call(
        owner_sum_kernel,
        out_shape=jax.ShapeDtypeStruct((32, 8, LANE), F32),
        in_specs=[VMEM],
        out_specs=VMEM,
        compiler_params=ROOM,
        name="owner_sum",
    )(got)
    got = lax.all_to_all(sent, ("y_lo", "y_hi", "x"), 0, 0, tiled=True)

    def by_row(value):
        return value.reshape(2, 16, LANE).transpose(1, 0, 2).reshape(32, LANE)

    def by_slot(value):
        return value.reshape(16, 2, LANE).transpose(1, 0, 2).reshape(2, BLOCK)

    state = jax.ShapeDtypeStruct((32, LANE), F32)
    new_master, new_first, new_second, sent = pl.pallas_call(
        adam_kernel,
        out_shape=(state, state, state, jax.ShapeDtypeStruct((48, 8, LANE), BF16)),
        in_specs=[VMEM] * 5,
        out_specs=(VMEM,) * 4,
        scratch_shapes=[pltpu.VMEM((32, LANE), F32)],
        compiler_params=ROOM,
        name="adam",
    )(got, signs, by_row(master), by_row(first_moment), by_row(second_moment))

    got = lax.all_to_all(sent, ("y_lo", "z"), 0, 0, tiled=True)
    sent = pl.pallas_call(
        repeat_kernel,
        out_shape=jax.ShapeDtypeStruct((4, 96, 512), BF16),
        in_specs=[VMEM],
        out_specs=VMEM,
        scratch_shapes=[pltpu.VMEM((384, LANE), F32)],
        compiler_params=ROOM,
        name="repeat",
    )(got.reshape(384, LANE))
    got = lax.all_to_all(sent, "x", 0, 0, tiled=True)
    got = lax.all_gather(got.reshape(384, 512), "core", axis=0, tiled=True).reshape(2, 4, 96, 512)

    params = pl.pallas_call(
        params_kernel,
        out_shape=jax.ShapeDtypeStruct((BLOCKS, BLOCK), BF16),
        in_specs=[VMEM] * 2,
        out_specs=HBM,
        scratch_shapes=[pltpu.VMEM((BLOCKS, BLOCK), BF16), pltpu.SemaphoreType.DMA((4,))],
        compiler_params=ROOM,
        name="params",
    )(place, got)
    return by_slot(new_master), by_slot(new_first), by_slot(new_second), params


def solution(mesh):
    fine = Mesh(np.asarray(mesh.devices).reshape(SIZES), AXES)
    group = ("y_lo", "z", "core")
    placed = (
        P(AXES, None, None),
        P(),
        P(),
        P(),
        P(group, None),
        P(group, None),
        P(group, None),
    )
    return jax.shard_map(
        on_device,
        mesh=fine,
        in_specs=placed,
        out_specs=(P(group, None), P(group, None), P(group, None), P()),
        check_vma=False,
    )
```

```python
import math

import jax
import jax.numpy as jnp
import numpy as np
from jax import lax
from jax.experimental import pallas as pl
from jax.experimental.pallas import tpu as pltpu
from jax.sharding import Mesh, PartitionSpec as P

beta_one = 0.9
beta_two = 0.95
first_fix = 1.0 - math.exp(100.0 * math.log(0.9))
second_fix = 1.0 - math.exp(100.0 * math.log(0.95))
learn_rate = 0.25
weight_decay = 0.1
epsilon = 1e-08

AXES = ("y_lo", "z", "core", "y_hi", "x")
SIZES = (4, 12, 2, 2, 4)
BLOCKS = 192
BLOCK = 2048
LANE = 128
INV_ROOT = 1.0 / math.sqrt(BLOCK)
F32 = jnp.float32
BF16 = jnp.bfloat16


def iota(shape, axis):
    return lax.broadcasted_iota(jnp.int32, shape, axis)


def parity_sign(both, bits):
    for shift in bits:
        both = both ^ jnp.right_shift(both, shift)
    return (1 - 2 * (both & 1)).astype(F32)


def rotate_kernel(
    order_hbm, rows_hbm, cols_hbm, grad_hbm, out_ref, signs_ref, place_ref, order_ref, rows_ref, cols_ref, grad_ref, mixed_ref, sems
):
    small = [
        pltpu.make_async_copy(order_hbm, order_ref, sems.at[0]),
        pltpu.make_async_copy(rows_hbm, rows_ref, sems.at[1]),
        pltpu.make_async_copy(cols_hbm, cols_ref, sems.at[2]),
    ]
    large = pltpu.make_async_copy(grad_hbm, grad_ref, sems.at[3])
    for copy in small:
        copy.start()
    large.start()
    core = lax.axis_index("core")
    own = ((lax.axis_index("y_lo") * 12 + lax.axis_index("z")) * 2 + core) * 2
    row = iota((BLOCKS, BLOCKS), 0)
    lane = iota((BLOCKS, BLOCKS), 1)
    half = (row >= 96).astype(jnp.int32)
    place = row - 96 * half
    y_lo = jnp.right_shift(place, 1) & 3
    z = jnp.right_shift(place, 3)
    owner = jnp.where(half == 1, core, 1 - core)
    slot = ((y_lo * 12 + z) * 2 + owner) * 2 + (place & 1)
    table = parity_sign(iota((256, 256), 0) & iota((256, 256), 1), (4, 2, 1)).astype(BF16)
    spread = jnp.where(iota((32, 16), 1) == jnp.right_shift(iota((32, 16), 0), 1), 1.0, 0.0).astype(BF16)
    core_of = (lane >= 96).astype(jnp.int32)
    rest = lane - 96 * core_of
    j_of = (rest >= 48).astype(jnp.int32)
    slot_of = ((rest - 48 * j_of) * 2 + core_of) * 2 + j_of
    scatter = jnp.where(row == slot_of, 1.0, 0.0).astype(BF16)
    for copy in small:
        copy.wait()
    order = order_ref[...].astype(F32)
    block = jnp.sum(jnp.where(slot == lane, order, 0.0), axis=1, keepdims=True)
    pick = jnp.where(block == lane.astype(F32), 1.0, 0.0).astype(BF16)
    row_bits = (2 * rows_ref[...] - 1).astype(F32).astype(BF16)
    col_bits = (2 * cols_ref[...] - 1).astype(F32).astype(BF16)
    row_signs = lax.dot_general(pick, row_bits, (((1,), (1,)), ((), ())), preferred_element_type=F32)
    col_signs = jnp.dot(pick, col_bits, preferred_element_type=F32)

    wanted = iota((32, BLOCKS), 1) == own + (iota((32, BLOCKS), 0) & 1)
    own_block = jnp.sum(jnp.where(wanted, order, 0.0), axis=1, keepdims=True)
    own_pick = jnp.where(own_block == iota((32, BLOCKS), 1).astype(F32), 1.0, 0.0)
    wide = jnp.dot(spread, row_bits, preferred_element_type=F32)
    own_rows = jnp.sum(wide * own_pick, axis=1, keepdims=True)
    signs_ref[...] = own_rows * jnp.dot(own_pick.astype(BF16), col_bits, preferred_element_type=F32)
    orders = jnp.broadcast_to(order, (8, BLOCKS)).astype(BF16)
    placed = jnp.dot(orders, scatter, preferred_element_type=F32)[0:1]
    place_ref[...] = jnp.where(row.astype(F32) == placed, 1.0, 0.0).astype(BF16)

    large.wait()
    picked = jnp.dot(pick, grad_ref[...], preferred_element_type=F32)
    signed = []
    for k in range(8):
        pair = [
            picked[:, a * LANE : (a + 1) * LANE] * col_signs * row_signs[:, a : a + 1] for a in (2 * k, 2 * k + 1)
        ]
        signed.append(jnp.concatenate(pair, axis=1).astype(BF16))
    product = jnp.dot(jnp.concatenate(signed, axis=0), table, preferred_element_type=F32)
    for k in range(8):
        mixed_ref[k] = product[k * BLOCKS : (k + 1) * BLOCKS]
    for start in range(0, BLOCKS, 16):
        mixed = [mixed_ref[k, start : start + 16] for k in range(8)]
        for span in (1, 2, 4):
            for k in range(8):
                if not k & span:
                    low, high = mixed[k], mixed[k + span]
                    mixed[k], mixed[k + span] = low + high, low - high
        for k in range(8):
            rotated = (mixed[k] * INV_ROOT).astype(BF16)
            out_ref[start // 96, k // 2, start % 96 : start % 96 + 16, (k % 2) * 256 : (k % 2) * 256 + 256] = rotated


def owner_sum_kernel(got_ref, out_ref):
    total = got_ref[0].astype(F32)
    for z in range(1, 12):
        total = total + got_ref[z].astype(F32)
    for y_lo in range(4):
        piece = jnp.concatenate(
            [total[2 * y_lo : 2 * y_lo + 2, a * LANE : (a + 1) * LANE] for a in range(4)], axis=0
        )
        for member in range(8):
            out_ref[8 * y_lo + member] = piece


def adam_kernel(got_ref, signs_ref, master_ref, first_ref, second_ref, new_master_ref, new_first_ref, new_second_ref, sent_ref, held_ref):
    total = got_ref[0:4]
    for y in range(1, 8):
        total = total + got_ref[4 * y : 4 * y + 4]
    gradient = total.reshape(32, LANE)
    new_first = beta_one * first_ref[...] + (1.0 - beta_one) * gradient
    new_second = beta_two * second_ref[...] + (1.0 - beta_two) * gradient * gradient
    new_first_ref[...] = new_first
    new_second_ref[...] = new_second
    update = new_first / first_fix / (jnp.sqrt(new_second / second_fix) + epsilon)
    row, col = iota((32, 32), 0), iota((32, 32), 1)
    same = ((row ^ col) & 1) == 0
    sub = jnp.where(same, parity_sign(jnp.right_shift(row & col, 1), (2, 1)), 0.0)
    table = parity_sign(iota((LANE, LANE), 0) & iota((LANE, LANE), 1), (4, 2, 1))
    restored = jnp.dot(sub, update, precision=lax.Precision.HIGHEST, preferred_element_type=F32)
    restored = jnp.dot(restored, table, precision=lax.Precision.HIGHEST, preferred_element_type=F32)
    restored = restored * INV_ROOT * signs_ref[...]
    master = master_ref[...]
    new_master = master - learn_rate * (restored + weight_decay * master)
    new_master_ref[...] = new_master
    held_ref[...] = new_master
    start = pl.multiple_of(lax.axis_index("x") * 8, 8)
    mine = held_ref[pl.ds(start, 8), :].astype(BF16)
    for member in range(48):
        sent_ref[member] = mine


def repeat_kernel(got_ref, out_ref, wide_ref):
    wide_ref[...] = got_ref[...].astype(F32)
    for a in range(4):
        rows = jnp.concatenate(
            [wide_ref[pl.ds(2 * a + j, 48, stride=8), :] for j in range(2)], axis=0
        ).astype(BF16)
        for x in range(4):
            out_ref[x, :, a * LANE : (a + 1) * LANE] = rows


def params_kernel(
    place_ref, got_ref, master_ref, first_ref, second_ref, out_hbm, master_hbm, first_hbm, second_hbm, out_ref, sems
):
    copies = [
        pltpu.make_async_copy(master_ref, master_hbm, sems.at[4]),
        pltpu.make_async_copy(first_ref, first_hbm, sems.at[5]),
        pltpu.make_async_copy(second_ref, second_hbm, sems.at[6]),
    ]
    for copy in copies:
        copy.start()
    for x in range(4):
        rows = jnp.concatenate([got_ref[0, x], got_ref[1, x]], axis=0)
        column = x * 512
        placed = jnp.dot(place_ref[...], rows, preferred_element_type=F32)
        out_ref[:, column : column + 512] = placed.astype(BF16)
        copy = pltpu.make_async_copy(
            out_ref.at[:, column : column + 512], out_hbm.at[:, column : column + 512], sems.at[x]
        )
        copy.start()
        copies.append(copy)
    for copy in copies:
        copy.wait()


VMEM = pl.BlockSpec(memory_space=pltpu.VMEM)
HBM = pl.BlockSpec(memory_space=pltpu.HBM)
ROOM = pltpu.CompilerParams(vmem_limit_bytes=32 * 1024 * 1024)


def on_device(grads, sign_rows, sign_cols, block_order, master, first_moment, second_moment):
    core = lax.axis_index("core")
    order_row = block_order.reshape(1, BLOCKS)
    rows_t = sign_rows.T

    halves, signs, place = pl.pallas_call(
        rotate_kernel,
        out_shape=(
            jax.ShapeDtypeStruct((2, 4, 96, 512), BF16),
            jax.ShapeDtypeStruct((32, LANE), F32),
            jax.ShapeDtypeStruct((BLOCKS, BLOCKS), BF16),
        ),
        in_specs=[HBM] * 4,
        out_specs=(VMEM,) * 3,
        scratch_shapes=[
            pltpu.VMEM((1, BLOCKS), jnp.int32),
            pltpu.VMEM((16, BLOCKS), jnp.int32),
            pltpu.VMEM((BLOCKS, LANE), jnp.int32),
            pltpu.VMEM((BLOCKS, BLOCK), BF16),
            pltpu.VMEM((8, BLOCKS, 256), F32),
            pltpu.SemaphoreType.DMA((4,)),
        ],
        compiler_params=ROOM,
        name="rotate",
    )(*(pltpu.with_memory_space_constraint(each, pltpu.HBM) for each in (order_row, rows_t, sign_cols, grads[0])))
    got = lax.all_gather(halves[0].reshape(384, 512), "core", axis=0, tiled=True).reshape(2, 4, 96, 512)
    other = lax.dynamic_index_in_dim(got, 1 - core, 0, keepdims=False)
    part = (halves[1].astype(F32) + other.astype(F32)).astype(BF16)
    got = lax.all_to_all(part, "x", 0, 0, tiled=True)
    part = jnp.sum(got.astype(F32), axis=0).astype(BF16)
    got = lax.all_to_all(part.reshape(12, 8, 512), "z", 0, 0, tiled=True)
    sent = pl.pallas_call(
        owner_sum_kernel,
        out_shape=jax.ShapeDtypeStruct((32, 8, LANE), F32),
        in_specs=[VMEM],
        out_specs=VMEM,
        compiler_params=ROOM,
        name="owner_sum",
    )(got)
    got = lax.all_to_all(sent, ("y_lo", "y_hi", "x"), 0, 0, tiled=True)

    def by_row(value):
        return value.reshape(2, 16, LANE).transpose(1, 0, 2).reshape(32, LANE)

    def by_slot(value):
        return value.reshape(16, 2, LANE).transpose(1, 0, 2).reshape(2, BLOCK)

    kept = pltpu.VMEM((32, LANE), F32)
    *states, sent = pl.pallas_call(
        adam_kernel,
        out_shape=(kept, kept, kept, jax.ShapeDtypeStruct((48, 8, LANE), BF16)),
        in_specs=[VMEM] * 5,
        out_specs=(VMEM,) * 4,
        scratch_shapes=[pltpu.VMEM((32, LANE), F32)],
        compiler_params=ROOM,
        name="adam",
    )(got, signs, by_row(master), by_row(first_moment), by_row(second_moment))

    got = lax.all_to_all(sent, ("y_lo", "z"), 0, 0, tiled=True)
    sent = pl.pallas_call(
        repeat_kernel,
        out_shape=jax.ShapeDtypeStruct((4, 96, 512), BF16),
        in_specs=[VMEM],
        out_specs=VMEM,
        scratch_shapes=[pltpu.VMEM((384, LANE), F32)],
        compiler_params=ROOM,
        name="repeat",
    )(got.reshape(384, LANE))
    got = lax.all_to_all(sent, "x", 0, 0, tiled=True)
    got = lax.all_gather(got.reshape(384, 512), "core", axis=0, tiled=True).reshape(2, 4, 96, 512)

    state = jax.ShapeDtypeStruct((32, LANE), F32)
    params, *states = pl.pallas_call(
        params_kernel,
        out_shape=(jax.ShapeDtypeStruct((BLOCKS, BLOCK), BF16), state, state, state),
        in_specs=[VMEM] * 5,
        out_specs=(HBM,) * 4,
        scratch_shapes=[pltpu.VMEM((BLOCKS, BLOCK), BF16), pltpu.SemaphoreType.DMA((7,))],
        compiler_params=ROOM,
        name="params",
    )(place, got, *states)
    return *(by_slot(state) for state in states), params


def solution(mesh):
    fine = Mesh(np.asarray(mesh.devices).reshape(SIZES), AXES)
    group = ("y_lo", "z", "core")
    placed = (
        P(AXES, None, None),
        P(),
        P(),
        P(),
        P(group, None),
        P(group, None),
        P(group, None),
    )
    return jax.shard_map(
        on_device,
        mesh=fine,
        in_specs=placed,
        out_specs=(P(group, None), P(group, None), P(group, None), P()),
        check_vma=False,
    )
```

```python
import math

import jax
import jax.numpy as jnp
import numpy as np
from jax import lax
from jax.experimental import pallas as pl
from jax.experimental.pallas import tpu as pltpu
from jax.sharding import Mesh, PartitionSpec as P

beta_one = 0.9
beta_two = 0.95
first_fix = 1.0 - math.exp(100.0 * math.log(0.9))
second_fix = 1.0 - math.exp(100.0 * math.log(0.95))
learn_rate = 0.25
weight_decay = 0.1
epsilon = 1e-08

AXES = ("y_lo", "z", "core", "y_hi", "x")
SIZES = (4, 12, 2, 2, 4)
BLOCKS = 192
BLOCK = 2048
LANE = 128
INV_ROOT = 1.0 / math.sqrt(BLOCK)
F32 = jnp.float32
BF16 = jnp.bfloat16


def iota(shape, axis):
    return lax.broadcasted_iota(jnp.int32, shape, axis)


def parity_sign(both, bits):
    for shift in bits:
        both = both ^ jnp.right_shift(both, shift)
    return (1 - 2 * (both & 1)).astype(F32)


def rotate_kernel(
    order_hbm, rows_hbm, cols_hbm, grad_hbm, out_ref, signs_ref, place_ref, order_ref, rows_ref, cols_ref, grad_ref, mixed_ref, sems
):
    small = [
        pltpu.make_async_copy(order_hbm, order_ref, sems.at[0]),
        pltpu.make_async_copy(rows_hbm, rows_ref, sems.at[1]),
        pltpu.make_async_copy(cols_hbm, cols_ref, sems.at[2]),
    ]
    large = pltpu.make_async_copy(grad_hbm, grad_ref, sems.at[3])
    for copy in small:
        copy.start()
    large.start()
    core = lax.axis_index("core")
    own = ((lax.axis_index("y_lo") * 12 + lax.axis_index("z")) * 2 + core) * 2
    row = iota((BLOCKS, BLOCKS), 0)
    lane = iota((BLOCKS, BLOCKS), 1)
    half = (row >= 96).astype(jnp.int32)
    place = row - 96 * half
    y_lo = sum((place >= bound).astype(jnp.int32) for bound in (24, 48, 72))
    z = jnp.right_shift(place - 24 * y_lo, 1)
    owner = jnp.where(half == 1, core, 1 - core)
    slot = ((y_lo * 12 + z) * 2 + owner) * 2 + (place & 1)
    table = parity_sign(iota((256, 256), 0) & iota((256, 256), 1), (4, 2, 1)).astype(BF16)
    spread = jnp.where(iota((32, 16), 1) == jnp.right_shift(iota((32, 16), 0), 1), 1.0, 0.0).astype(BF16)
    core_of = (lane >= 96).astype(jnp.int32)
    rest = lane - 96 * core_of
    j_of = (rest >= 48).astype(jnp.int32)
    slot_of = ((rest - 48 * j_of) * 2 + core_of) * 2 + j_of
    scatter = jnp.where(row == slot_of, 1.0, 0.0).astype(BF16)
    for copy in small:
        copy.wait()
    order = order_ref[...].astype(F32)
    block = jnp.sum(jnp.where(slot == lane, order, 0.0), axis=1, keepdims=True)
    pick = jnp.where(block == lane.astype(F32), 1.0, 0.0).astype(BF16)
    row_bits = (2 * rows_ref[...] - 1).astype(F32).astype(BF16)
    col_bits = (2 * cols_ref[...] - 1).astype(F32).astype(BF16)
    row_signs = lax.dot_general(pick, row_bits, (((1,), (1,)), ((), ())), preferred_element_type=F32)
    col_signs = jnp.dot(pick, col_bits, preferred_element_type=F32)

    wanted = iota((32, BLOCKS), 1) == own + (iota((32, BLOCKS), 0) & 1)
    own_block = jnp.sum(jnp.where(wanted, order, 0.0), axis=1, keepdims=True)
    own_pick = jnp.where(own_block == iota((32, BLOCKS), 1).astype(F32), 1.0, 0.0)
    wide = jnp.dot(spread, row_bits, preferred_element_type=F32)
    own_rows = jnp.sum(wide * own_pick, axis=1, keepdims=True)
    signs_ref[...] = own_rows * jnp.dot(own_pick.astype(BF16), col_bits, preferred_element_type=F32)
    orders = jnp.broadcast_to(order, (8, BLOCKS)).astype(BF16)
    placed = jnp.dot(orders, scatter, preferred_element_type=F32)[0:1]
    place_ref[...] = jnp.where(row.astype(F32) == placed, 1.0, 0.0).astype(BF16)

    large.wait()
    picked = jnp.dot(pick, grad_ref[...], preferred_element_type=F32)
    signed = []
    for k in range(8):
        pair = [
            picked[:, a * LANE : (a + 1) * LANE] * col_signs * row_signs[:, a : a + 1] for a in (2 * k, 2 * k + 1)
        ]
        signed.append(jnp.concatenate(pair, axis=1).astype(BF16))
    product = jnp.dot(jnp.concatenate(signed, axis=0), table, preferred_element_type=F32)
    for k in range(8):
        mixed_ref[k] = product[k * BLOCKS : (k + 1) * BLOCKS]
    for start in range(0, BLOCKS, 24):
        mixed = [mixed_ref[k, start : start + 24] for k in range(8)]
        for span in (1, 2, 4):
            for k in range(8):
                if not k & span:
                    low, high = mixed[k], mixed[k + span]
                    mixed[k], mixed[k + span] = low + high, low - high
        for x in range(4):
            pair = mixed[2 * x], mixed[2 * x + 1]
            rows = [part[:, c : c + LANE] * INV_ROOT for part in pair for c in (0, LANE)]
            out_ref[start // 96, (start % 96) // 24 * 4 + x] = jnp.concatenate(rows, axis=0).astype(BF16)


def plane_sum_kernel(got_ref, out_ref):
    total = got_ref[0].astype(F32)
    for member in range(1, 16):
        total = total + got_ref[member].astype(F32)
    for z in range(12):
        rows = [total[24 * a + 2 * z : 24 * a + 2 * z + 2] for a in range(4)]
        piece = jnp.concatenate(rows, axis=0).astype(BF16)
        for member in range(8):
            out_ref[8 * z + member] = piece


def adam_kernel(got_ref, signs_ref, master_ref, first_ref, second_ref, new_master_ref, new_first_ref, new_second_ref, sent_ref, held_ref):
    total = got_ref[0:4].astype(F32)
    for source in range(1, 24):
        total = total + got_ref[4 * source : 4 * source + 4].astype(F32)
    gradient = total.reshape(32, LANE)
    new_first = beta_one * first_ref[...] + (1.0 - beta_one) * gradient
    new_second = beta_two * second_ref[...] + (1.0 - beta_two) * gradient * gradient
    new_first_ref[...] = new_first
    new_second_ref[...] = new_second
    update = new_first / first_fix / (jnp.sqrt(new_second / second_fix) + epsilon)
    row, col = iota((32, 32), 0), iota((32, 32), 1)
    same = ((row ^ col) & 1) == 0
    sub = jnp.where(same, parity_sign(jnp.right_shift(row & col, 1), (2, 1)), 0.0)
    table = parity_sign(iota((LANE, LANE), 0) & iota((LANE, LANE), 1), (4, 2, 1))
    restored = jnp.dot(sub, update, precision=lax.Precision.HIGHEST, preferred_element_type=F32)
    restored = jnp.dot(restored, table, precision=lax.Precision.HIGHEST, preferred_element_type=F32)
    restored = restored * INV_ROOT * signs_ref[...]
    master = master_ref[...]
    new_master = master - learn_rate * (restored + weight_decay * master)
    new_master_ref[...] = new_master
    held_ref[...] = new_master
    start = pl.multiple_of(lax.axis_index("x") * 8, 8)
    mine = held_ref[pl.ds(start, 8), :].astype(BF16)
    for member in range(48):
        sent_ref[member] = mine


def repeat_kernel(got_ref, out_ref, wide_ref):
    wide_ref[...] = got_ref[...].astype(F32)
    for a in range(4):
        rows = jnp.concatenate(
            [wide_ref[pl.ds(2 * a + j, 48, stride=8), :] for j in range(2)], axis=0
        ).astype(BF16)
        for x in range(4):
            out_ref[x, :, a * LANE : (a + 1) * LANE] = rows


def params_kernel(
    place_ref, got_ref, master_ref, first_ref, second_ref, out_hbm, master_hbm, first_hbm, second_hbm, out_ref, sems
):
    copies = [
        pltpu.make_async_copy(master_ref, master_hbm, sems.at[4]),
        pltpu.make_async_copy(first_ref, first_hbm, sems.at[5]),
        pltpu.make_async_copy(second_ref, second_hbm, sems.at[6]),
    ]
    for copy in copies:
        copy.start()
    for x in range(4):
        rows = jnp.concatenate([got_ref[0, x], got_ref[1, x]], axis=0)
        column = x * 512
        placed = jnp.dot(place_ref[...], rows, preferred_element_type=F32)
        out_ref[:, column : column + 512] = placed.astype(BF16)
        copy = pltpu.make_async_copy(
            out_ref.at[:, column : column + 512], out_hbm.at[:, column : column + 512], sems.at[x]
        )
        copy.start()
        copies.append(copy)
    for copy in copies:
        copy.wait()


VMEM = pl.BlockSpec(memory_space=pltpu.VMEM)
HBM = pl.BlockSpec(memory_space=pltpu.HBM)
ROOM = pltpu.CompilerParams(vmem_limit_bytes=32 * 1024 * 1024)


def on_device(grads, sign_rows, sign_cols, block_order, master, first_moment, second_moment):
    core = lax.axis_index("core")
    order_row = block_order.reshape(1, BLOCKS)
    rows_t = sign_rows.T

    halves, signs, place = pl.pallas_call(
        rotate_kernel,
        out_shape=(
            jax.ShapeDtypeStruct((2, 16, 96, LANE), BF16),
            jax.ShapeDtypeStruct((32, LANE), F32),
            jax.ShapeDtypeStruct((BLOCKS, BLOCKS), BF16),
        ),
        in_specs=[HBM] * 4,
        out_specs=(VMEM,) * 3,
        scratch_shapes=[
            pltpu.VMEM((1, BLOCKS), jnp.int32),
            pltpu.VMEM((16, BLOCKS), jnp.int32),
            pltpu.VMEM((BLOCKS, LANE), jnp.int32),
            pltpu.VMEM((BLOCKS, BLOCK), BF16),
            pltpu.VMEM((8, BLOCKS, 256), F32),
            pltpu.SemaphoreType.DMA((4,)),
        ],
        compiler_params=ROOM,
        name="rotate",
    )(*(pltpu.with_memory_space_constraint(each, pltpu.HBM) for each in (order_row, rows_t, sign_cols, grads[0])))
    got = lax.all_gather(halves[0].reshape(1536, LANE), "core", axis=0, tiled=True).reshape(2, 16, 96, LANE)
    other = lax.dynamic_index_in_dim(got, 1 - core, 0, keepdims=False)
    part = (halves[1].astype(F32) + other.astype(F32)).astype(BF16)
    got = lax.all_to_all(part, ("y_lo", "x"), 0, 0, tiled=True)
    sent = pl.pallas_call(
        plane_sum_kernel,
        out_shape=jax.ShapeDtypeStruct((96, 8, LANE), BF16),
        in_specs=[VMEM],
        out_specs=VMEM,
        compiler_params=ROOM,
        name="plane_sum",
    )(got)
    got = lax.all_to_all(sent, ("z", "y_hi", "x"), 0, 0, tiled=True)

    def by_row(value):
        return value.reshape(2, 16, LANE).transpose(1, 0, 2).reshape(32, LANE)

    def by_slot(value):
        return value.reshape(16, 2, LANE).transpose(1, 0, 2).reshape(2, BLOCK)

    kept = pltpu.VMEM((32, LANE), F32)
    *states, sent = pl.pallas_call(
        adam_kernel,
        out_shape=(kept, kept, kept, jax.ShapeDtypeStruct((48, 8, LANE), BF16)),
        in_specs=[VMEM] * 5,
        out_specs=(VMEM,) * 4,
        scratch_shapes=[pltpu.VMEM((32, LANE), F32)],
        compiler_params=ROOM,
        name="adam",
    )(got, signs, by_row(master), by_row(first_moment), by_row(second_moment))

    got = lax.all_to_all(sent, ("y_lo", "z"), 0, 0, tiled=True)
    sent = pl.pallas_call(
        repeat_kernel,
        out_shape=jax.ShapeDtypeStruct((4, 96, 512), BF16),
        in_specs=[VMEM],
        out_specs=VMEM,
        scratch_shapes=[pltpu.VMEM((384, LANE), F32)],
        compiler_params=ROOM,
        name="repeat",
    )(got.reshape(384, LANE))
    got = lax.all_to_all(sent, "x", 0, 0, tiled=True)
    got = lax.all_gather(got.reshape(384, 512), "core", axis=0, tiled=True).reshape(2, 4, 96, 512)

    state = jax.ShapeDtypeStruct((32, LANE), F32)
    params, *states = pl.pallas_call(
        params_kernel,
        out_shape=(jax.ShapeDtypeStruct((BLOCKS, BLOCK), BF16), state, state, state),
        in_specs=[VMEM] * 5,
        out_specs=(HBM,) * 4,
        scratch_shapes=[pltpu.VMEM((BLOCKS, BLOCK), BF16), pltpu.SemaphoreType.DMA((7,))],
        compiler_params=ROOM,
        name="params",
    )(place, got, *states)
    return *(by_slot(state) for state in states), params


def solution(mesh):
    fine = Mesh(np.asarray(mesh.devices).reshape(SIZES), AXES)
    group = ("y_lo", "z", "core")
    placed = (
        P(AXES, None, None),
        P(),
        P(),
        P(),
        P(group, None),
        P(group, None),
        P(group, None),
    )
    return jax.shard_map(
        on_device,
        mesh=fine,
        in_specs=placed,
        out_specs=(P(group, None), P(group, None), P(group, None), P()),
        check_vma=False,
    )
```

```python
import math

import jax
import jax.numpy as jnp
import numpy as np
from jax import lax
from jax.experimental import pallas as pl
from jax.experimental.pallas import tpu as pltpu
from jax.sharding import Mesh, PartitionSpec as P

beta_one = 0.9
beta_two = 0.95
first_fix = 1.0 - math.exp(100.0 * math.log(0.9))
second_fix = 1.0 - math.exp(100.0 * math.log(0.95))
learn_rate = 0.25
weight_decay = 0.1
epsilon = 1e-08

AXES = ("y_lo", "z", "core", "y_hi", "x")
SIZES = (4, 12, 2, 2, 4)
BLOCKS = 192
BLOCK = 2048
LANE = 128
INV_ROOT = 1.0 / math.sqrt(BLOCK)
F32 = jnp.float32
BF16 = jnp.bfloat16


def iota(shape, axis):
    return lax.broadcasted_iota(jnp.int32, shape, axis)


def parity_sign(both, bits):
    for shift in bits:
        both = both ^ jnp.right_shift(both, shift)
    return (1 - 2 * (both & 1)).astype(F32)


def rotate_kernel(
    order_hbm, rows_hbm, cols_hbm, grad_hbm, out_ref, signs_ref, place_ref, order_ref, rows_ref, cols_ref, grad_ref, mixed_ref, sems
):
    small = [
        pltpu.make_async_copy(order_hbm, order_ref, sems.at[0]),
        pltpu.make_async_copy(rows_hbm, rows_ref, sems.at[1]),
        pltpu.make_async_copy(cols_hbm, cols_ref, sems.at[2]),
    ]
    large = pltpu.make_async_copy(grad_hbm, grad_ref, sems.at[3])
    for copy in small:
        copy.start()
    large.start()
    core = lax.axis_index("core")
    row = iota((BLOCKS, BLOCKS), 0)
    lane = iota((BLOCKS, BLOCKS), 1)
    half = (row >= 96).astype(jnp.int32)
    place = row - 96 * half
    y_lo = sum((place >= bound).astype(jnp.int32) for bound in (24, 48, 72))
    z = jnp.right_shift(place - 24 * y_lo, 1)
    owner = jnp.where(half == 1, core, 1 - core)
    slot = ((y_lo * 12 + z) * 2 + owner) * 2 + (place & 1)
    table = parity_sign(iota((256, 256), 0) & iota((256, 256), 1), (4, 2, 1)).astype(BF16)
    spread = jnp.where(iota((32, 16), 1) == jnp.right_shift(iota((32, 16), 0), 1), 1.0, 0.0).astype(BF16)
    wide_lane = iota((BLOCKS, 384), 1)
    core_of = (wide_lane >= 192).astype(jnp.int32)
    rest = wide_lane - 192 * core_of
    y_of = sum((rest >= bound).astype(jnp.int32) for bound in (48, 96, 144))
    rest = rest - 48 * y_of
    parity = (rest >= 24).astype(jnp.int32)
    rest = rest - 24 * parity
    slot_of = ((y_of * 12 + jnp.right_shift(rest, 1)) * 2 + core_of) * 2 + (rest & 1)
    wide_row = iota((BLOCKS, 384), 0)
    scatter = jnp.where(wide_row == slot_of, 1.0, 0.0).astype(BF16)
    for copy in small:
        copy.wait()
    order = order_ref[...].astype(F32)
    block = jnp.sum(jnp.where(slot == lane, order, 0.0), axis=1, keepdims=True)
    pick = jnp.where(block == lane.astype(F32), 1.0, 0.0).astype(BF16)
    row_bits = (2 * rows_ref[...] - 1).astype(F32).astype(BF16)
    col_bits = (2 * cols_ref[...] - 1).astype(F32).astype(BF16)
    row_signs = lax.dot_general(pick, row_bits, (((1,), (1,)), ((), ())), preferred_element_type=F32)
    col_signs = jnp.dot(pick, col_bits, preferred_element_type=F32)

    wide = jnp.dot(spread, row_bits, preferred_element_type=F32)
    for i, axis in enumerate(("x", "y_lo")):
        own = ((lax.axis_index(axis) * 12 + lax.axis_index("z")) * 2 + core) * 2
        wanted = iota((32, BLOCKS), 1) == own + (iota((32, BLOCKS), 0) & 1)
        own_block = jnp.sum(jnp.where(wanted, order, 0.0), axis=1, keepdims=True)
        own_pick = jnp.where(own_block == iota((32, BLOCKS), 1).astype(F32), 1.0, 0.0)
        own_rows = jnp.sum(wide * own_pick, axis=1, keepdims=True)
        signs_ref[i] = own_rows * jnp.dot(own_pick.astype(BF16), col_bits, preferred_element_type=F32)
    orders = jnp.broadcast_to(order, (8, BLOCKS)).astype(BF16)
    placed = jnp.dot(orders, scatter, preferred_element_type=F32)[0:1]
    match = wide_row.astype(F32) == placed
    for i in range(2):
        place_ref[i] = jnp.where(match & (parity == i), 1.0, 0.0).astype(BF16)

    large.wait()
    picked = jnp.dot(pick, grad_ref[...], preferred_element_type=F32)
    signed = []
    for k in range(8):
        pair = [
            picked[:, a * LANE : (a + 1) * LANE] * col_signs * row_signs[:, a : a + 1] for a in (2 * k, 2 * k + 1)
        ]
        signed.append(jnp.concatenate(pair, axis=1).astype(BF16))
    product = jnp.dot(jnp.concatenate(signed, axis=0), table, preferred_element_type=F32)
    for k in range(8):
        mixed_ref[k] = product[k * BLOCKS : (k + 1) * BLOCKS]
    for start in range(0, BLOCKS, 24):
        mixed = [mixed_ref[k, start : start + 24] for k in range(8)]
        for span in (1, 2, 4):
            for k in range(8):
                if not k & span:
                    low, high = mixed[k], mixed[k + span]
                    mixed[k], mixed[k + span] = low + high, low - high
        for x in range(4):
            pair = mixed[2 * x], mixed[2 * x + 1]
            rows = [part[:, c : c + LANE] * INV_ROOT for part in pair for c in (0, LANE)]
            out_ref[start // 96, (start % 96) // 24 * 4 + x] = jnp.concatenate(rows, axis=0).astype(BF16)


def x_sum_kernel(got_ref, out_ref):
    total = got_ref[0].astype(F32)
    for x in range(1, 4):
        total = total + got_ref[x].astype(F32)
    for z in range(12):
        rows = [total[24 * a + 2 * z : 24 * a + 2 * z + 2] for a in range(16)]
        out_ref[z] = jnp.concatenate(rows, axis=0).astype(BF16)


def z_sum_kernel(got_ref, out_ref):
    total = got_ref[0].astype(F32)
    for z in range(1, 12):
        total = total + got_ref[z].astype(F32)
    for y in range(8):
        out_ref[y] = total


def adam_step(gradient, signs, master, first, second):
    new_first = beta_one * first + (1.0 - beta_one) * gradient
    new_second = beta_two * second + (1.0 - beta_two) * gradient * gradient
    update = new_first / first_fix / (jnp.sqrt(new_second / second_fix) + epsilon)
    row, col = iota((32, 32), 0), iota((32, 32), 1)
    same = ((row ^ col) & 1) == 0
    sub = jnp.where(same, parity_sign(jnp.right_shift(row & col, 1), (2, 1)), 0.0)
    table = parity_sign(iota((LANE, LANE), 0) & iota((LANE, LANE), 1), (4, 2, 1))
    restored = jnp.dot(sub, update, precision=lax.Precision.HIGHEST, preferred_element_type=F32)
    restored = jnp.dot(restored, table, precision=lax.Precision.HIGHEST, preferred_element_type=F32)
    restored = restored * INV_ROOT * signs
    new_master = master - learn_rate * (restored + weight_decay * master)
    return new_master, new_first, new_second


def adam_kernel(got_ref, signs_ref, state_ref, sent_ref, terms_ref):
    gradient = got_ref[0]
    for y in range(1, 8):
        gradient = gradient + got_ref[y]
    new_master, _, _ = adam_step(gradient, signs_ref[0], state_ref[0], state_ref[1], state_ref[2])
    mine = new_master.astype(BF16)
    for z in range(12):
        sent_ref[z] = mine
    for i in range(3):
        term = gradient.astype(BF16)
        terms_ref[i] = term
        gradient = gradient - term.astype(F32)


def repeat_kernel(got_ref, terms_ref, out_ref):
    wide = [got_ref[z].astype(F32) for z in range(12)]
    for pair in range(8):
        rows = [wide[z][2 * a : 2 * a + 2] for a in (2 * pair, 2 * pair + 1) for z in range(12)]
        piece = jnp.concatenate(rows, axis=0).astype(BF16)
        for x in range(4):
            out_ref[x, 48 * pair : 48 * pair + 48] = piece
    for i in range(3):
        for x in range(4):
            out_ref[x, 384 + 32 * i : 416 + 32 * i] = terms_ref[i]


def params_kernel(
    place_ref, got_ref, signs_ref, state_ref, out_hbm, master_hbm, first_hbm, second_hbm, out_ref, new_ref, sems
):
    rows = jnp.concatenate(
        [
            jnp.concatenate(
                [got_ref[c, y, 48 * pair : 48 * pair + 48] for c in range(2) for y in range(4)], axis=0
            )
            for pair in range(8)
        ],
        axis=1,
    )
    copies = []
    for half in range(2):
        part = rows[:, 512 * half : 512 * half + 512]
        for i in range(2):
            placed = jnp.dot(place_ref[i], part, preferred_element_type=F32).astype(BF16)
            for k in range(4):
                column = (8 * half + 2 * k + i) * LANE
                out_ref[:, column : column + LANE] = placed[:, k * LANE : (k + 1) * LANE]
        columns = slice(1024 * half, 1024 * half + 1024)
        copies.append(pltpu.make_async_copy(out_ref.at[:, columns], out_hbm.at[:, columns], sems.at[half]))
        copies[-1].start()
    terms = got_ref.at[lax.axis_index("core"), lax.axis_index("y_lo")]
    gradient = terms[384:416].astype(F32) + terms[416:448].astype(F32) + terms[448:480].astype(F32)
    news = adam_step(gradient, signs_ref[1], state_ref[0], state_ref[1], state_ref[2])
    for i, target in enumerate((master_hbm, first_hbm, second_hbm)):
        new_ref[i] = news[i]
        copies.append(pltpu.make_async_copy(new_ref.at[i], target, sems.at[2 + i]))
        copies[-1].start()
    for copy in copies:
        copy.wait()


VMEM = pl.BlockSpec(memory_space=pltpu.VMEM)
HBM = pl.BlockSpec(memory_space=pltpu.HBM)
ROOM = pltpu.CompilerParams(vmem_limit_bytes=32 * 1024 * 1024)


def on_device(grads, sign_rows, sign_cols, block_order, master, first_moment, second_moment):
    core = lax.axis_index("core")
    order_row = block_order.reshape(1, BLOCKS)
    rows_t = sign_rows.T

    def by_row(value):
        return value.reshape(2, 16, LANE).transpose(1, 0, 2).reshape(32, LANE)

    def by_slot(value):
        return value.reshape(16, 2, LANE).transpose(1, 0, 2).reshape(2, BLOCK)

    state = jnp.stack([by_row(each) for each in (master, first_moment, second_moment)])
    mine = jnp.where(lax.axis_index("y_lo") == lax.axis_index("x"), state, 0.0)
    lent = lax.psum_scatter(jnp.broadcast_to(mine, (4, 3, 32, LANE)), "y_lo", scatter_dimension=0)

    halves, signs, place = pl.pallas_call(
        rotate_kernel,
        out_shape=(
            jax.ShapeDtypeStruct((2, 16, 96, LANE), BF16),
            jax.ShapeDtypeStruct((2, 32, LANE), F32),
            jax.ShapeDtypeStruct((2, BLOCKS, 384), BF16),
        ),
        in_specs=[HBM] * 4,
        out_specs=(VMEM,) * 3,
        scratch_shapes=[
            pltpu.VMEM((1, BLOCKS), jnp.int32),
            pltpu.VMEM((16, BLOCKS), jnp.int32),
            pltpu.VMEM((BLOCKS, LANE), jnp.int32),
            pltpu.VMEM((BLOCKS, BLOCK), BF16),
            pltpu.VMEM((8, BLOCKS, 256), F32),
            pltpu.SemaphoreType.DMA((4,)),
        ],
        compiler_params=ROOM,
        name="rotate",
    )(*(pltpu.with_memory_space_constraint(each, pltpu.HBM) for each in (order_row, rows_t, sign_cols, grads[0])))
    got = lax.all_gather(halves[0].reshape(1536, LANE), "core", axis=0, tiled=True).reshape(2, 16, 96, LANE)
    other = lax.dynamic_index_in_dim(got, 1 - core, 0, keepdims=False)
    part = (halves[1].astype(F32) + other.astype(F32)).astype(BF16)
    got = lax.all_to_all(part.reshape(4, 384, LANE), "x", 0, 0, tiled=True)

    def local(kernel, name, out_shape, *operands):
        return pl.pallas_call(
            kernel,
            out_shape=out_shape,
            in_specs=[VMEM] * len(operands),
            out_specs=jax.tree.map(lambda _: VMEM, out_shape),
            compiler_params=ROOM,
            name=name,
        )(*operands)

    sent = local(x_sum_kernel, "x_sum", jax.ShapeDtypeStruct((12, 32, LANE), BF16), got)
    got = lax.all_to_all(sent, "z", 0, 0, tiled=True)
    sent = local(z_sum_kernel, "z_sum", jax.ShapeDtypeStruct((8, 32, LANE), F32), got)
    got = lax.all_to_all(sent, ("y_lo", "y_hi"), 0, 0, tiled=True)
    shapes = (jax.ShapeDtypeStruct((12, 32, LANE), BF16), jax.ShapeDtypeStruct((3, 32, LANE), BF16))
    sent, terms = local(adam_kernel, "adam", shapes, got, signs, lent)
    got = lax.all_to_all(sent, "z", 0, 0, tiled=True)
    sent = local(repeat_kernel, "repeat", jax.ShapeDtypeStruct((4, 480, LANE), BF16), got, terms)
    got = lax.all_to_all(sent, "x", 0, 0, tiled=True)
    got = lax.all_gather(got.reshape(1920, LANE), "core", axis=0, tiled=True).reshape(2, 4, 480, LANE)

    kept = jax.ShapeDtypeStruct((32, LANE), F32)
    params, *news = pl.pallas_call(
        params_kernel,
        out_shape=(jax.ShapeDtypeStruct((BLOCKS, BLOCK), BF16), kept, kept, kept),
        in_specs=[VMEM] * 4,
        out_specs=(HBM,) * 4,
        scratch_shapes=[
            pltpu.VMEM((BLOCKS, BLOCK), BF16),
            pltpu.VMEM((3, 32, LANE), F32),
            pltpu.SemaphoreType.DMA((5,)),
        ],
        compiler_params=ROOM,
        name="params",
    )(place, got, signs, state)
    return *(by_slot(new) for new in news), params


def solution(mesh):
    fine = Mesh(np.asarray(mesh.devices).reshape(SIZES), AXES)
    group = ("y_lo", "z", "core")
    placed = (
        P(AXES, None, None),
        P(),
        P(),
        P(),
        P(group, None),
        P(group, None),
        P(group, None),
    )
    return jax.shard_map(
        on_device,
        mesh=fine,
        in_specs=placed,
        out_specs=(P(group, None), P(group, None), P(group, None), P()),
        check_vma=False,
    )
```

```python
import math

import jax
import jax.numpy as jnp
import numpy as np
from jax import lax
from jax.experimental import pallas as pl
from jax.experimental.pallas import tpu as pltpu
from jax.sharding import Mesh, PartitionSpec as P

beta_one = 0.9
beta_two = 0.95
first_fix = 1.0 - math.exp(100.0 * math.log(0.9))
second_fix = 1.0 - math.exp(100.0 * math.log(0.95))
learn_rate = 0.25
weight_decay = 0.1
epsilon = 1e-08

AXES = ("y_lo", "z", "core", "y_hi", "x")
SIZES = (4, 12, 2, 2, 4)
BLOCKS = 192
BLOCK = 2048
LANE = 128
INV_ROOT = 1.0 / math.sqrt(BLOCK)
F32 = jnp.float32
BF16 = jnp.bfloat16


def iota(shape, axis):
    return lax.broadcasted_iota(jnp.int32, shape, axis)


def parity_sign(both, bits):
    for shift in bits:
        both = both ^ jnp.right_shift(both, shift)
    return (1 - 2 * (both & 1)).astype(F32)


def rotate_kernel(
    order_hbm, rows_hbm, cols_hbm, grad_hbm, out_ref, signs_ref, place_ref, order_ref, rows_ref, cols_ref, grad_ref, mixed_ref, sems
):
    small = [
        pltpu.make_async_copy(order_hbm, order_ref, sems.at[0]),
        pltpu.make_async_copy(rows_hbm, rows_ref, sems.at[1]),
        pltpu.make_async_copy(cols_hbm, cols_ref, sems.at[2]),
    ]
    large = pltpu.make_async_copy(grad_hbm, grad_ref, sems.at[3])
    for copy in small:
        copy.start()
    large.start()
    core = lax.axis_index("core")
    row = iota((BLOCKS, BLOCKS), 0)
    lane = iota((BLOCKS, BLOCKS), 1)
    half = (row >= 96).astype(jnp.int32)
    place = row - 96 * half
    y_lo = sum((place >= bound).astype(jnp.int32) for bound in (24, 48, 72))
    z = jnp.right_shift(place - 24 * y_lo, 1)
    owner = jnp.where(half == 1, core, 1 - core)
    slot = ((y_lo * 12 + z) * 2 + owner) * 2 + (place & 1)
    table = parity_sign(iota((256, 256), 0) & iota((256, 256), 1), (4, 2, 1)).astype(BF16)
    spread = jnp.where(iota((32, 16), 1) == jnp.right_shift(iota((32, 16), 0), 1), 1.0, 0.0).astype(BF16)
    wide_lane = iota((BLOCKS, 384), 1)
    core_of = (wide_lane >= 192).astype(jnp.int32)
    rest = wide_lane - 192 * core_of
    y_of = sum((rest >= bound).astype(jnp.int32) for bound in (48, 96, 144))
    rest = rest - 48 * y_of
    parity = (rest >= 24).astype(jnp.int32)
    rest = rest - 24 * parity
    slot_of = ((y_of * 12 + jnp.right_shift(rest, 1)) * 2 + core_of) * 2 + (rest & 1)
    wide_row = iota((BLOCKS, 384), 0)
    scatter = jnp.where(wide_row == slot_of, 1.0, 0.0).astype(BF16)
    for copy in small:
        copy.wait()
    order = order_ref[...].astype(F32)
    block = jnp.sum(jnp.where(slot == lane, order, 0.0), axis=1, keepdims=True)
    pick = jnp.where(block == lane.astype(F32), 1.0, 0.0).astype(BF16)
    row_bits = (2 * rows_ref[...] - 1).astype(F32).astype(BF16)
    col_bits = (2 * cols_ref[...] - 1).astype(F32).astype(BF16)
    row_signs = lax.dot_general(pick, row_bits, (((1,), (1,)), ((), ())), preferred_element_type=F32)
    col_signs = jnp.dot(pick, col_bits, preferred_element_type=F32)

    wide = jnp.dot(spread, row_bits, preferred_element_type=F32)
    for i, axis in enumerate(("x", "y_lo")):
        own = ((lax.axis_index(axis) * 12 + lax.axis_index("z")) * 2 + core) * 2
        wanted = iota((32, BLOCKS), 1) == own + (iota((32, BLOCKS), 0) & 1)
        own_block = jnp.sum(jnp.where(wanted, order, 0.0), axis=1, keepdims=True)
        own_pick = jnp.where(own_block == iota((32, BLOCKS), 1).astype(F32), 1.0, 0.0)
        own_rows = jnp.sum(wide * own_pick, axis=1, keepdims=True)
        signs_ref[i] = own_rows * jnp.dot(own_pick.astype(BF16), col_bits, preferred_element_type=F32)
    orders = jnp.broadcast_to(order, (8, BLOCKS)).astype(BF16)
    placed = jnp.dot(orders, scatter, preferred_element_type=F32)[0:1]
    match = wide_row.astype(F32) == placed
    for i in range(2):
        place_ref[i] = jnp.where(match & (parity == i), 1.0, 0.0).astype(BF16)

    large.wait()
    picked = jnp.dot(pick, grad_ref[...], preferred_element_type=F32)
    signed = []
    for k in range(8):
        pair = [
            picked[:, a * LANE : (a + 1) * LANE] * col_signs * row_signs[:, a : a + 1] for a in (2 * k, 2 * k + 1)
        ]
        signed.append(jnp.concatenate(pair, axis=1).astype(BF16))
    product = jnp.dot(jnp.concatenate(signed, axis=0), table, preferred_element_type=F32)
    for k in range(8):
        mixed_ref[k] = product[k * BLOCKS : (k + 1) * BLOCKS]
    for start in range(0, BLOCKS, 24):
        mixed = [mixed_ref[k, start : start + 24] for k in range(8)]
        for span in (1, 2, 4):
            for k in range(8):
                if not k & span:
                    low, high = mixed[k], mixed[k + span]
                    mixed[k], mixed[k + span] = low + high, low - high
        for x in range(4):
            pair = mixed[2 * x], mixed[2 * x + 1]
            rows = [part[:, c : c + LANE] * INV_ROOT for part in pair for c in (0, LANE)]
            out_ref[start // 96, (start % 96) // 24 * 4 + x] = jnp.concatenate(rows, axis=0).astype(BF16)


def x_sum_kernel(got_ref, out_ref):
    total = got_ref[0].astype(F32)
    for x in range(1, 4):
        total = total + got_ref[x].astype(F32)
    for z in range(12):
        rows = [total[24 * a + 2 * z : 24 * a + 2 * z + 2] for a in range(16)]
        out_ref[z] = jnp.concatenate(rows, axis=0).astype(BF16)


def z_sum_kernel(got_ref, out_ref):
    total = got_ref[0].astype(F32)
    for z in range(1, 12):
        total = total + got_ref[z].astype(F32)
    for y in range(8):
        out_ref[y] = total


def adam_step(gradient, signs, master, first, second):
    new_first = beta_one * first + (1.0 - beta_one) * gradient
    new_second = beta_two * second + (1.0 - beta_two) * gradient * gradient
    update = new_first / first_fix / (jnp.sqrt(new_second / second_fix) + epsilon)
    row, col = iota((32, 32), 0), iota((32, 32), 1)
    same = ((row ^ col) & 1) == 0
    sub = jnp.where(same, parity_sign(jnp.right_shift(row & col, 1), (2, 1)), 0.0)
    table = parity_sign(iota((LANE, LANE), 0) & iota((LANE, LANE), 1), (4, 2, 1))
    restored = jnp.dot(sub, update, precision=lax.Precision.HIGHEST, preferred_element_type=F32)
    restored = jnp.dot(restored, table, precision=lax.Precision.HIGHEST, preferred_element_type=F32)
    restored = restored * INV_ROOT * signs
    new_master = master - learn_rate * (restored + weight_decay * master)
    return new_master, new_first, new_second


def adam_kernel(got_ref, signs_ref, state_ref, sent_ref, terms_ref):
    gradient = got_ref[0]
    for y in range(1, 8):
        gradient = gradient + got_ref[y]
    new_master, _, _ = adam_step(gradient, signs_ref[0], state_ref[0], state_ref[1], state_ref[2])
    mine = new_master.astype(BF16)
    for z in range(12):
        sent_ref[z] = mine
    for i in range(3):
        term = gradient.astype(BF16)
        terms_ref[i] = term
        gradient = gradient - term.astype(F32)


def repeat_kernel(got_ref, terms_ref, out_ref):
    wide = [got_ref[z].astype(F32) for z in range(12)]
    for pair in range(8):
        rows = [wide[z][2 * a : 2 * a + 2] for a in (2 * pair, 2 * pair + 1) for z in range(12)]
        piece = jnp.concatenate(rows, axis=0).astype(BF16)
        for x in range(4):
            out_ref[x, 48 * pair : 48 * pair + 48] = piece
    for i in range(3):
        for x in range(4):
            out_ref[x, 384 + 32 * i : 416 + 32 * i] = terms_ref[i]


def params_kernel(
    place_ref, got_ref, signs_ref, state_ref, out_hbm, master_hbm, first_hbm, second_hbm, out_ref, new_ref, sems
):
    rows = jnp.concatenate(
        [
            jnp.concatenate(
                [got_ref[c, y, 48 * pair : 48 * pair + 48] for c in range(2) for y in range(4)], axis=0
            )
            for pair in range(8)
        ],
        axis=1,
    )
    copies = []
    for half in range(2):
        part = rows[:, 512 * half : 512 * half + 512]
        for i in range(2):
            placed = jnp.dot(place_ref[i], part, preferred_element_type=F32).astype(BF16)
            for k in range(4):
                column = (8 * half + 2 * k + i) * LANE
                out_ref[:, column : column + LANE] = placed[:, k * LANE : (k + 1) * LANE]
        columns = slice(1024 * half, 1024 * half + 1024)
        copies.append(pltpu.make_async_copy(out_ref.at[:, columns], out_hbm.at[:, columns], sems.at[half]))
        copies[-1].start()
    terms = got_ref.at[lax.axis_index("core"), lax.axis_index("y_lo")]
    gradient = terms[384:416].astype(F32) + terms[416:448].astype(F32) + terms[448:480].astype(F32)
    news = adam_step(gradient, signs_ref[1], state_ref[0], state_ref[1], state_ref[2])
    for i, target in enumerate((master_hbm, first_hbm, second_hbm)):
        new_ref[i] = news[i]
        copies.append(pltpu.make_async_copy(new_ref.at[i], target, sems.at[2 + i]))
        copies[-1].start()
    for copy in copies:
        copy.wait()


VMEM = pl.BlockSpec(memory_space=pltpu.VMEM)
HBM = pl.BlockSpec(memory_space=pltpu.HBM)
ROOM = pltpu.CompilerParams(vmem_limit_bytes=32 * 1024 * 1024)


def on_device(grads, sign_rows, sign_cols, block_order, master, first_moment, second_moment):
    core = lax.axis_index("core")
    order_row = block_order.reshape(1, BLOCKS)
    rows_t = sign_rows.T

    def by_row(value):
        return value.reshape(2, 16, LANE).transpose(1, 0, 2).reshape(32, LANE)

    def by_slot(value):
        return value.reshape(16, 2, LANE).transpose(1, 0, 2).reshape(2, BLOCK)

    state = jnp.stack([by_row(each) for each in (master, first_moment, second_moment)])

    halves, signs, place = pl.pallas_call(
        rotate_kernel,
        out_shape=(
            jax.ShapeDtypeStruct((2, 16, 96, LANE), BF16),
            jax.ShapeDtypeStruct((2, 32, LANE), F32),
            jax.ShapeDtypeStruct((2, BLOCKS, 384), BF16),
        ),
        in_specs=[HBM] * 4,
        out_specs=(VMEM,) * 3,
        scratch_shapes=[
            pltpu.VMEM((1, BLOCKS), jnp.int32),
            pltpu.VMEM((16, BLOCKS), jnp.int32),
            pltpu.VMEM((BLOCKS, LANE), jnp.int32),
            pltpu.VMEM((BLOCKS, BLOCK), BF16),
            pltpu.VMEM((8, BLOCKS, 256), F32),
            pltpu.SemaphoreType.DMA((4,)),
        ],
        compiler_params=ROOM,
        name="rotate",
    )(*(pltpu.with_memory_space_constraint(each, pltpu.HBM) for each in (order_row, rows_t, sign_cols, grads[0])))
    got = lax.all_gather(halves[0].reshape(1536, LANE), "core", axis=0, tiled=True).reshape(2, 16, 96, LANE)
    other = lax.dynamic_index_in_dim(got, 1 - core, 0, keepdims=False)
    part = (halves[1].astype(F32) + other.astype(F32)).astype(BF16)
    got = lax.all_to_all(part.reshape(4, 384, LANE), "x", 0, 0, tiled=True)

    def local(kernel, name, out_shape, *operands):
        return pl.pallas_call(
            kernel,
            out_shape=out_shape,
            in_specs=[VMEM] * len(operands),
            out_specs=jax.tree.map(lambda _: VMEM, out_shape),
            compiler_params=ROOM,
            name=name,
        )(*operands)

    sent = local(x_sum_kernel, "x_sum", jax.ShapeDtypeStruct((12, 32, LANE), BF16), got)
    sent, state = lax.optimization_barrier((sent, state))
    swap = [(4 * y_lo + x, 4 * x + y_lo) for y_lo in range(4) for x in range(4)]
    lent = lax.ppermute(state, ("y_lo", "x"), swap)
    got = lax.all_to_all(sent, "z", 0, 0, tiled=True)
    sent = local(z_sum_kernel, "z_sum", jax.ShapeDtypeStruct((8, 32, LANE), F32), got)
    got = lax.all_to_all(sent, ("y_lo", "y_hi"), 0, 0, tiled=True)
    shapes = (jax.ShapeDtypeStruct((12, 32, LANE), BF16), jax.ShapeDtypeStruct((3, 32, LANE), BF16))
    sent, terms = local(adam_kernel, "adam", shapes, got, signs, lent)
    got = lax.all_to_all(sent, "z", 0, 0, tiled=True)
    sent = local(repeat_kernel, "repeat", jax.ShapeDtypeStruct((4, 480, LANE), BF16), got, terms)
    got = lax.all_to_all(sent, "x", 0, 0, tiled=True)
    got = lax.all_gather(got.reshape(1920, LANE), "core", axis=0, tiled=True).reshape(2, 4, 480, LANE)

    kept = jax.ShapeDtypeStruct((32, LANE), F32)
    params, *news = pl.pallas_call(
        params_kernel,
        out_shape=(jax.ShapeDtypeStruct((BLOCKS, BLOCK), BF16), kept, kept, kept),
        in_specs=[VMEM] * 4,
        out_specs=(HBM,) * 4,
        scratch_shapes=[
            pltpu.VMEM((BLOCKS, BLOCK), BF16),
            pltpu.VMEM((3, 32, LANE), F32),
            pltpu.SemaphoreType.DMA((5,)),
        ],
        compiler_params=ROOM,
        name="params",
    )(place, got, signs, state)
    return *(by_slot(new) for new in news), params


def solution(mesh):
    fine = Mesh(np.asarray(mesh.devices).reshape(SIZES), AXES)
    group = ("y_lo", "z", "core")
    placed = (
        P(AXES, None, None),
        P(),
        P(),
        P(),
        P(group, None),
        P(group, None),
        P(group, None),
    )
    return jax.shard_map(
        on_device,
        mesh=fine,
        in_specs=placed,
        out_specs=(P(group, None), P(group, None), P(group, None), P()),
        check_vma=False,
    )
```

```python
import math

import jax
import jax.numpy as jnp
import numpy as np
from jax import lax
from jax.experimental import pallas as pl
from jax.experimental.pallas import tpu as pltpu
from jax.sharding import Mesh, PartitionSpec as P

beta_one = 0.9
beta_two = 0.95
first_fix = 1.0 - math.exp(100.0 * math.log(0.9))
second_fix = 1.0 - math.exp(100.0 * math.log(0.95))
learn_rate = 0.25
weight_decay = 0.1
epsilon = 1e-08

AXES = ("y_lo", "z", "core", "y_hi", "x")
SIZES = (4, 12, 2, 2, 4)
BLOCKS = 192
BLOCK = 2048
LANE = 128
INV_ROOT = 1.0 / math.sqrt(BLOCK)
F32 = jnp.float32
BF16 = jnp.bfloat16


def iota(shape, axis):
    return lax.broadcasted_iota(jnp.int32, shape, axis)


def parity_sign(both, bits):
    for shift in bits:
        both = both ^ jnp.right_shift(both, shift)
    return (1 - 2 * (both & 1)).astype(F32)


def rotate_kernel(
    order_hbm, rows_hbm, cols_hbm, grad_hbm, out_ref, signs_ref, place_ref, order_ref, rows_ref, cols_ref, grad_ref, mixed_ref, sems
):
    small = [
        pltpu.make_async_copy(order_hbm, order_ref, sems.at[0]),
        pltpu.make_async_copy(rows_hbm, rows_ref, sems.at[1]),
        pltpu.make_async_copy(cols_hbm, cols_ref, sems.at[2]),
    ]
    large = pltpu.make_async_copy(grad_hbm, grad_ref, sems.at[3])
    for copy in small:
        copy.start()
    large.start()
    core = lax.axis_index("core")
    row = iota((BLOCKS, BLOCKS), 0)
    lane = iota((BLOCKS, BLOCKS), 1)
    half = (row >= 96).astype(jnp.int32)
    place = row - 96 * half
    y_lo = sum((place >= bound).astype(jnp.int32) for bound in (24, 48, 72))
    z = jnp.right_shift(place - 24 * y_lo, 1)
    owner = jnp.where(half == 1, core, 1 - core)
    slot = ((y_lo * 12 + z) * 2 + owner) * 2 + (place & 1)
    table = parity_sign(iota((256, 256), 0) & iota((256, 256), 1), (4, 2, 1)).astype(BF16)
    spread = jnp.where(iota((32, 16), 1) == jnp.right_shift(iota((32, 16), 0), 1), 1.0, 0.0).astype(BF16)
    wide_lane = iota((BLOCKS, 384), 1)
    core_of = (wide_lane >= 192).astype(jnp.int32)
    rest = wide_lane - 192 * core_of
    y_of = sum((rest >= bound).astype(jnp.int32) for bound in (48, 96, 144))
    rest = rest - 48 * y_of
    parity = (rest >= 24).astype(jnp.int32)
    rest = rest - 24 * parity
    slot_of = ((y_of * 12 + jnp.right_shift(rest, 1)) * 2 + core_of) * 2 + (rest & 1)
    wide_row = iota((BLOCKS, 384), 0)
    scatter = jnp.where(wide_row == slot_of, 1.0, 0.0).astype(BF16)
    for copy in small:
        copy.wait()
    order = order_ref[...].astype(F32)
    block = jnp.sum(jnp.where(slot == lane, order, 0.0), axis=1, keepdims=True)
    pick = jnp.where(block == lane.astype(F32), 1.0, 0.0).astype(BF16)
    row_bits = (2 * rows_ref[...] - 1).astype(F32).astype(BF16)
    col_bits = (2 * cols_ref[...] - 1).astype(F32).astype(BF16)
    row_signs = lax.dot_general(pick, row_bits, (((1,), (1,)), ((), ())), preferred_element_type=F32)
    col_signs = jnp.dot(pick, col_bits, preferred_element_type=F32)

    wide = jnp.dot(spread, row_bits, preferred_element_type=F32)
    for i, axis in enumerate(("x", "y_lo")):
        own = ((lax.axis_index(axis) * 12 + lax.axis_index("z")) * 2 + core) * 2
        wanted = iota((32, BLOCKS), 1) == own + (iota((32, BLOCKS), 0) & 1)
        own_block = jnp.sum(jnp.where(wanted, order, 0.0), axis=1, keepdims=True)
        own_pick = jnp.where(own_block == iota((32, BLOCKS), 1).astype(F32), 1.0, 0.0)
        own_rows = jnp.sum(wide * own_pick, axis=1, keepdims=True)
        signs_ref[i] = own_rows * jnp.dot(own_pick.astype(BF16), col_bits, preferred_element_type=F32)
    orders = jnp.broadcast_to(order, (8, BLOCKS)).astype(BF16)
    placed = jnp.dot(orders, scatter, preferred_element_type=F32)[0:1]
    match = wide_row.astype(F32) == placed
    for i in range(2):
        place_ref[i] = jnp.where(match & (parity == i), 1.0, 0.0).astype(BF16)

    large.wait()
    picked = jnp.dot(pick, grad_ref[...], preferred_element_type=F32)
    signed = []
    for k in range(8):
        pair = [
            picked[:, a * LANE : (a + 1) * LANE] * col_signs * row_signs[:, a : a + 1] for a in (2 * k, 2 * k + 1)
        ]
        signed.append(jnp.concatenate(pair, axis=1).astype(BF16))
    product = jnp.dot(jnp.concatenate(signed, axis=0), table, preferred_element_type=F32)
    for k in range(8):
        mixed_ref[k] = product[k * BLOCKS : (k + 1) * BLOCKS]
    for start in range(0, BLOCKS, 24):
        mixed = [mixed_ref[k, start : start + 24] for k in range(8)]
        for span in (1, 2, 4):
            for k in range(8):
                if not k & span:
                    low, high = mixed[k], mixed[k + span]
                    mixed[k], mixed[k + span] = low + high, low - high
        for x in range(4):
            pair = mixed[2 * x], mixed[2 * x + 1]
            rows = [part[:, c : c + LANE] * INV_ROOT for part in pair for c in (0, LANE)]
            out_ref[start // 96, (start % 96) // 24 * 4 + x] = jnp.concatenate(rows, axis=0).astype(BF16)


def x_sum_kernel(got_ref, out_ref):
    total = got_ref[0].astype(F32)
    for x in range(1, 4):
        total = total + got_ref[x].astype(F32)
    for z in range(12):
        rows = [total[24 * a + 2 * z : 24 * a + 2 * z + 2] for a in range(16)]
        out_ref[z] = jnp.concatenate(rows, axis=0).astype(BF16)


def z_sum_kernel(got_ref, out_ref):
    total = got_ref[0].astype(F32)
    for z in range(1, 12):
        total = total + got_ref[z].astype(F32)
    for y in range(8):
        out_ref[y] = total


def adam_step(gradient, signs, master, first, second):
    new_first = beta_one * first + (1.0 - beta_one) * gradient
    new_second = beta_two * second + (1.0 - beta_two) * gradient * gradient
    update = new_first / first_fix / (jnp.sqrt(new_second / second_fix) + epsilon)
    row, col = iota((32, 32), 0), iota((32, 32), 1)
    same = ((row ^ col) & 1) == 0
    sub = jnp.where(same, parity_sign(jnp.right_shift(row & col, 1), (2, 1)), 0.0)
    table = parity_sign(iota((LANE, LANE), 0) & iota((LANE, LANE), 1), (4, 2, 1))
    restored = jnp.dot(sub, update, precision=lax.Precision.HIGHEST, preferred_element_type=F32)
    restored = jnp.dot(restored, table, precision=lax.Precision.HIGHEST, preferred_element_type=F32)
    restored = restored * INV_ROOT * signs
    new_master = master - learn_rate * (restored + weight_decay * master)
    return new_master, new_first, new_second


def adam_kernel(got_ref, signs_ref, state_ref, sent_ref, terms_ref):
    gradient = got_ref[0]
    for y in range(1, 8):
        gradient = gradient + got_ref[y]
    new_master, _, _ = adam_step(gradient, signs_ref[0], state_ref[0], state_ref[1], state_ref[2])
    mine = new_master.astype(BF16)
    for z in range(12):
        sent_ref[z] = mine
    for i in range(3):
        term = gradient.astype(BF16)
        terms_ref[i] = term
        gradient = gradient - term.astype(F32)


def repeat_kernel(got_ref, terms_ref, out_ref):
    wide = [got_ref[z].astype(F32) for z in range(12)]
    for pair in range(8):
        rows = [wide[z][2 * a : 2 * a + 2] for a in (2 * pair, 2 * pair + 1) for z in range(12)]
        piece = jnp.concatenate(rows, axis=0).astype(BF16)
        for x in range(4):
            out_ref[x, 48 * pair : 48 * pair + 48] = piece
    for i in range(3):
        for x in range(4):
            out_ref[x, 384 + 32 * i : 416 + 32 * i] = terms_ref[i]


def params_kernel(
    place_ref, got_ref, signs_ref, state_ref, out_hbm, master_hbm, first_hbm, second_hbm, out_ref, new_ref, sems
):
    rows = jnp.concatenate(
        [
            jnp.concatenate(
                [got_ref[c, y, 48 * pair : 48 * pair + 48] for c in range(2) for y in range(4)], axis=0
            )
            for pair in range(8)
        ],
        axis=1,
    )
    copies = []
    for half in range(2):
        part = rows[:, 512 * half : 512 * half + 512]
        for i in range(2):
            placed = jnp.dot(place_ref[i], part, preferred_element_type=F32).astype(BF16)
            for k in range(4):
                column = (8 * half + 2 * k + i) * LANE
                out_ref[:, column : column + LANE] = placed[:, k * LANE : (k + 1) * LANE]
        columns = slice(1024 * half, 1024 * half + 1024)
        copies.append(pltpu.make_async_copy(out_ref.at[:, columns], out_hbm.at[:, columns], sems.at[half]))
        copies[-1].start()
    terms = got_ref.at[lax.axis_index("core"), lax.axis_index("y_lo")]
    gradient = terms[384:416].astype(F32) + terms[416:448].astype(F32) + terms[448:480].astype(F32)
    news = adam_step(gradient, signs_ref[1], state_ref[0], state_ref[1], state_ref[2])
    for i, target in enumerate((master_hbm, first_hbm, second_hbm)):
        new_ref[i] = news[i]
        copies.append(pltpu.make_async_copy(new_ref.at[i], target, sems.at[2 + i]))
        copies[-1].start()
    for copy in copies:
        copy.wait()


VMEM = pl.BlockSpec(memory_space=pltpu.VMEM)
HBM = pl.BlockSpec(memory_space=pltpu.HBM)
ROOM = pltpu.CompilerParams(vmem_limit_bytes=32 * 1024 * 1024)


def on_device(grads, sign_rows, sign_cols, block_order, master, first_moment, second_moment):
    core = lax.axis_index("core")
    order_row = block_order.reshape(1, BLOCKS)
    rows_t = sign_rows.T

    def by_row(value):
        return value.reshape(2, 16, LANE).transpose(1, 0, 2).reshape(32, LANE)

    def by_slot(value):
        return value.reshape(16, 2, LANE).transpose(1, 0, 2).reshape(2, BLOCK)

    state = jnp.stack([by_row(each) for each in (master, first_moment, second_moment)])

    halves, signs, place = pl.pallas_call(
        rotate_kernel,
        out_shape=(
            jax.ShapeDtypeStruct((2, 16, 96, LANE), BF16),
            jax.ShapeDtypeStruct((2, 32, LANE), F32),
            jax.ShapeDtypeStruct((2, BLOCKS, 384), BF16),
        ),
        in_specs=[HBM] * 4,
        out_specs=(VMEM,) * 3,
        scratch_shapes=[
            pltpu.VMEM((1, BLOCKS), jnp.int32),
            pltpu.VMEM((16, BLOCKS), jnp.int32),
            pltpu.VMEM((BLOCKS, LANE), jnp.int32),
            pltpu.VMEM((BLOCKS, BLOCK), BF16),
            pltpu.VMEM((8, BLOCKS, 256), F32),
            pltpu.SemaphoreType.DMA((4,)),
        ],
        compiler_params=ROOM,
        name="rotate",
    )(*(pltpu.with_memory_space_constraint(each, pltpu.HBM) for each in (order_row, rows_t, sign_cols, grads[0])))
    got = lax.all_gather(halves[0].reshape(1536, LANE), "core", axis=0, tiled=True).reshape(2, 16, 96, LANE)
    other = lax.dynamic_index_in_dim(got, 1 - core, 0, keepdims=False)
    part = (halves[1].astype(F32) + other.astype(F32)).astype(BF16)
    part, state = lax.optimization_barrier((part, state))
    got = lax.all_to_all(part.reshape(4, 384, LANE), "x", 0, 0, tiled=True)

    def local(kernel, name, out_shape, *operands):
        return pl.pallas_call(
            kernel,
            out_shape=out_shape,
            in_specs=[VMEM] * len(operands),
            out_specs=jax.tree.map(lambda _: VMEM, out_shape),
            compiler_params=ROOM,
            name=name,
        )(*operands)

    sent = local(x_sum_kernel, "x_sum", jax.ShapeDtypeStruct((12, 32, LANE), BF16), got)
    sent, state = lax.optimization_barrier((sent, state))
    lend = []
    for x in range(4):
        for y in (x, x + 4):
            for up, right in ((2, 0), (1, 1), (-1, -1), (0, 2)):
                source, target = (y, (x + right) % 4), ((y + up) % 8, x)
                lend.append(tuple((row % 4 * 2 + row // 4) * 4 + column for row, column in (source, target)))
    lent = lax.ppermute(state, ("y_lo", "y_hi", "x"), lend)
    got = lax.all_to_all(sent, "z", 0, 0, tiled=True)
    sent = local(z_sum_kernel, "z_sum", jax.ShapeDtypeStruct((8, 32, LANE), F32), got)
    got = lax.all_to_all(sent, ("y_lo", "y_hi"), 0, 0, tiled=True)
    shapes = (jax.ShapeDtypeStruct((12, 32, LANE), BF16), jax.ShapeDtypeStruct((3, 32, LANE), BF16))
    sent, terms = local(adam_kernel, "adam", shapes, got, signs, lent)
    got = lax.all_to_all(sent, "z", 0, 0, tiled=True)
    sent = local(repeat_kernel, "repeat", jax.ShapeDtypeStruct((4, 480, LANE), BF16), got, terms)
    got = lax.all_to_all(sent, "x", 0, 0, tiled=True)
    got = lax.all_gather(got.reshape(1920, LANE), "core", axis=0, tiled=True).reshape(2, 4, 480, LANE)

    kept = jax.ShapeDtypeStruct((32, LANE), F32)
    params, *news = pl.pallas_call(
        params_kernel,
        out_shape=(jax.ShapeDtypeStruct((BLOCKS, BLOCK), BF16), kept, kept, kept),
        in_specs=[VMEM] * 4,
        out_specs=(HBM,) * 4,
        scratch_shapes=[
            pltpu.VMEM((BLOCKS, BLOCK), BF16),
            pltpu.VMEM((3, 32, LANE), F32),
            pltpu.SemaphoreType.DMA((5,)),
        ],
        compiler_params=ROOM,
        name="params",
    )(place, got, signs, state)
    return *(by_slot(new) for new in news), params


def solution(mesh):
    fine = Mesh(np.asarray(mesh.devices).reshape(SIZES), AXES)
    group = ("y_lo", "z", "core")
    placed = (
        P(AXES, None, None),
        P(),
        P(),
        P(),
        P(group, None),
        P(group, None),
        P(group, None),
    )
    return jax.shard_map(
        on_device,
        mesh=fine,
        in_specs=placed,
        out_specs=(P(group, None), P(group, None), P(group, None), P()),
        check_vma=False,
    )
```

```python
import math

import jax
import jax.numpy as jnp
import numpy as np
from jax import lax
from jax.experimental import pallas as pl
from jax.experimental.pallas import tpu as pltpu
from jax.sharding import Mesh, PartitionSpec as P

beta_one = 0.9
beta_two = 0.95
first_fix = 1.0 - math.exp(100.0 * math.log(0.9))
second_fix = 1.0 - math.exp(100.0 * math.log(0.95))
learn_rate = 0.25
weight_decay = 0.1
epsilon = 1e-08

AXES = ("y_lo", "z", "core", "y_hi", "x")
SIZES = (4, 12, 2, 2, 4)
BLOCKS = 192
BLOCK = 2048
LANE = 128
INV_ROOT = 1.0 / math.sqrt(BLOCK)
F32 = jnp.float32
BF16 = jnp.bfloat16


def iota(shape, axis):
    return lax.broadcasted_iota(jnp.int32, shape, axis)


def parity_sign(both, bits):
    for shift in bits:
        both = both ^ jnp.right_shift(both, shift)
    return (1 - 2 * (both & 1)).astype(F32)


def rotate_kernel(
    order_hbm, rows_hbm, cols_hbm, grad_hbm, master_hbm, first_hbm, second_hbm,
    out_ref, signs_ref, place_ref, state_ref, order_ref, rows_ref, cols_ref, grad_ref, mixed_ref, sems
):
    small = [
        pltpu.make_async_copy(order_hbm, order_ref, sems.at[0]),
        pltpu.make_async_copy(rows_hbm, rows_ref, sems.at[1]),
        pltpu.make_async_copy(cols_hbm, cols_ref, sems.at[2]),
    ]
    large = pltpu.make_async_copy(grad_hbm, grad_ref, sems.at[3])
    states = [
        pltpu.make_async_copy(each, state_ref.at[i], sems.at[4 + i])
        for i, each in enumerate((master_hbm, first_hbm, second_hbm))
    ]
    for copy in small + [large] + states:
        copy.start()
    core = lax.axis_index("core")
    row = iota((BLOCKS, BLOCKS), 0)
    lane = iota((BLOCKS, BLOCKS), 1)
    half = (row >= 96).astype(jnp.int32)
    place = row - 96 * half
    y_lo = sum((place >= bound).astype(jnp.int32) for bound in (24, 48, 72))
    z = jnp.right_shift(place - 24 * y_lo, 1)
    owner = jnp.where(half == 1, core, 1 - core)
    slot = ((y_lo * 12 + z) * 2 + owner) * 2 + (place & 1)
    table = parity_sign(iota((256, 256), 0) & iota((256, 256), 1), (4, 2, 1)).astype(BF16)
    spread = jnp.where(iota((32, 16), 1) == jnp.right_shift(iota((32, 16), 0), 1), 1.0, 0.0).astype(BF16)
    wide_lane = iota((BLOCKS, 384), 1)
    core_of = (wide_lane >= 192).astype(jnp.int32)
    rest = wide_lane - 192 * core_of
    y_of = sum((rest >= bound).astype(jnp.int32) for bound in (48, 96, 144))
    rest = rest - 48 * y_of
    parity = (rest >= 24).astype(jnp.int32)
    rest = rest - 24 * parity
    slot_of = ((y_of * 12 + jnp.right_shift(rest, 1)) * 2 + core_of) * 2 + (rest & 1)
    wide_row = iota((BLOCKS, 384), 0)
    scatter = jnp.where(wide_row == slot_of, 1.0, 0.0).astype(BF16)
    for copy in small:
        copy.wait()
    order = order_ref[...].astype(F32)
    block = jnp.sum(jnp.where(slot == lane, order, 0.0), axis=1, keepdims=True)
    pick = jnp.where(block == lane.astype(F32), 1.0, 0.0).astype(BF16)
    row_bits = (2 * rows_ref[...] - 1).astype(F32).astype(BF16)
    col_bits = (2 * cols_ref[...] - 1).astype(F32).astype(BF16)
    row_signs = lax.dot_general(pick, row_bits, (((1,), (1,)), ((), ())), preferred_element_type=F32)
    col_signs = jnp.dot(pick, col_bits, preferred_element_type=F32)

    wide = jnp.dot(spread, row_bits, preferred_element_type=F32)
    for i, axis in enumerate(("x", "y_lo")):
        own = ((lax.axis_index(axis) * 12 + lax.axis_index("z")) * 2 + core) * 2
        wanted = iota((32, BLOCKS), 1) == own + (iota((32, BLOCKS), 0) & 1)
        own_block = jnp.sum(jnp.where(wanted, order, 0.0), axis=1, keepdims=True)
        own_pick = jnp.where(own_block == iota((32, BLOCKS), 1).astype(F32), 1.0, 0.0)
        own_rows = jnp.sum(wide * own_pick, axis=1, keepdims=True)
        signs_ref[i] = own_rows * jnp.dot(own_pick.astype(BF16), col_bits, preferred_element_type=F32)
    orders = jnp.broadcast_to(order, (8, BLOCKS)).astype(BF16)
    placed = jnp.dot(orders, scatter, preferred_element_type=F32)[0:1]
    match = wide_row.astype(F32) == placed
    for i in range(2):
        place_ref[i] = jnp.where(match & (parity == i), 1.0, 0.0).astype(BF16)

    large.wait()
    picked = jnp.dot(pick, grad_ref[...], preferred_element_type=F32)
    signed = []
    for k in range(8):
        pair = [
            picked[:, a * LANE : (a + 1) * LANE] * col_signs * row_signs[:, a : a + 1] for a in (2 * k, 2 * k + 1)
        ]
        signed.append(jnp.concatenate(pair, axis=1).astype(BF16))
    product = jnp.dot(jnp.concatenate(signed, axis=0), table, preferred_element_type=F32)
    for k in range(8):
        mixed_ref[k] = product[k * BLOCKS : (k + 1) * BLOCKS]
    for start in range(0, BLOCKS, 24):
        mixed = [mixed_ref[k, start : start + 24] for k in range(8)]
        for span in (1, 2, 4):
            for k in range(8):
                if not k & span:
                    low, high = mixed[k], mixed[k + span]
                    mixed[k], mixed[k + span] = low + high, low - high
        for x in range(4):
            pair = mixed[2 * x], mixed[2 * x + 1]
            rows = [part[:, c : c + LANE] * INV_ROOT for part in pair for c in (0, LANE)]
            out_ref[start // 96, (start % 96) // 24 * 4 + x] = jnp.concatenate(rows, axis=0).astype(BF16)
    for copy in states:
        copy.wait()


def x_sum_kernel(got_ref, out_ref):
    total = got_ref[0].astype(F32)
    for x in range(1, 4):
        total = total + got_ref[x].astype(F32)
    for z in range(12):
        rows = [total[24 * a + 2 * z : 24 * a + 2 * z + 2] for a in range(16)]
        out_ref[z] = jnp.concatenate(rows, axis=0).astype(BF16)


def z_sum_kernel(got_ref, out_ref):
    total = got_ref[0].astype(F32)
    for z in range(1, 12):
        total = total + got_ref[z].astype(F32)
    for y in range(8):
        out_ref[y] = total


def adam_step(gradient, signs, master, first, second):
    new_first = beta_one * first + (1.0 - beta_one) * gradient
    new_second = beta_two * second + (1.0 - beta_two) * gradient * gradient
    update = new_first / first_fix / (jnp.sqrt(new_second / second_fix) + epsilon)
    row, col = iota((32, 32), 0), iota((32, 32), 1)
    same = ((row ^ col) & 1) == 0
    sub = jnp.where(same, parity_sign(jnp.right_shift(row & col, 1), (2, 1)), 0.0)
    table = parity_sign(iota((LANE, LANE), 0) & iota((LANE, LANE), 1), (4, 2, 1))
    restored = jnp.dot(sub, update, precision=lax.Precision.HIGHEST, preferred_element_type=F32)
    restored = jnp.dot(restored, table, precision=lax.Precision.HIGHEST, preferred_element_type=F32)
    restored = restored * INV_ROOT * signs
    new_master = master - learn_rate * (restored + weight_decay * master)
    return new_master, new_first, new_second


def adam_kernel(got_ref, signs_ref, state_ref, sent_ref, terms_ref):
    gradient = got_ref[0]
    for y in range(1, 8):
        gradient = gradient + got_ref[y]
    new_master, _, _ = adam_step(gradient, signs_ref[0], state_ref[0], state_ref[1], state_ref[2])
    mine = new_master.astype(BF16)
    for z in range(12):
        sent_ref[z] = mine
    for i in range(3):
        term = gradient.astype(BF16)
        terms_ref[i] = term
        gradient = gradient - term.astype(F32)


def repeat_kernel(got_ref, terms_ref, out_ref):
    wide = [got_ref[z].astype(F32) for z in range(12)]
    for pair in range(8):
        rows = [wide[z][2 * a : 2 * a + 2] for a in (2 * pair, 2 * pair + 1) for z in range(12)]
        piece = jnp.concatenate(rows, axis=0).astype(BF16)
        for x in range(4):
            out_ref[x, 48 * pair : 48 * pair + 48] = piece
    for i in range(3):
        for x in range(4):
            out_ref[x, 384 + 32 * i : 416 + 32 * i] = terms_ref[i]


def params_kernel(
    place_ref, got_ref, signs_ref, state_ref, out_hbm, master_hbm, first_hbm, second_hbm, out_ref, new_ref, sems
):
    rows = jnp.concatenate(
        [
            jnp.concatenate(
                [got_ref[c, y, 48 * pair : 48 * pair + 48] for c in range(2) for y in range(4)], axis=0
            )
            for pair in range(8)
        ],
        axis=1,
    )
    copies = []
    for quarter in range(4):
        part = rows[:, 256 * quarter : 256 * quarter + 256]
        for i in range(2):
            placed = jnp.dot(place_ref[i], part, preferred_element_type=F32).astype(BF16)
            for k in range(2):
                column = (4 * quarter + 2 * k + i) * LANE
                out_ref[:, column : column + LANE] = placed[:, k * LANE : (k + 1) * LANE]
        columns = slice(512 * quarter, 512 * quarter + 512)
        copies.append(pltpu.make_async_copy(out_ref.at[:, columns], out_hbm.at[:, columns], sems.at[quarter]))
        copies[-1].start()
    terms = got_ref.at[lax.axis_index("core"), lax.axis_index("y_lo")]
    gradient = terms[384:416].astype(F32) + terms[416:448].astype(F32) + terms[448:480].astype(F32)
    news = adam_step(gradient, signs_ref[1], state_ref[0], state_ref[1], state_ref[2])
    for i, target in enumerate((master_hbm, first_hbm, second_hbm)):
        new_ref[i] = news[i]
        copies.append(pltpu.make_async_copy(new_ref.at[i], target, sems.at[4 + i]))
        copies[-1].start()
    for copy in copies:
        copy.wait()


VMEM = pl.BlockSpec(memory_space=pltpu.VMEM)
HBM = pl.BlockSpec(memory_space=pltpu.HBM)
ROOM = pltpu.CompilerParams(vmem_limit_bytes=32 * 1024 * 1024)


def on_device(grads, sign_rows, sign_cols, block_order, master, first_moment, second_moment):
    core = lax.axis_index("core")
    order_row = block_order.reshape(1, BLOCKS)
    rows_t = sign_rows.T

    def by_row(value):
        return value.reshape(2, 16, LANE).transpose(1, 0, 2).reshape(32, LANE)

    def by_slot(value):
        return value.reshape(16, 2, LANE).transpose(1, 0, 2).reshape(2, BLOCK)

    inputs = order_row, rows_t, sign_cols, grads[0], by_row(master), by_row(first_moment), by_row(second_moment)
    halves, signs, place, state = pl.pallas_call(
        rotate_kernel,
        out_shape=(
            jax.ShapeDtypeStruct((2, 16, 96, LANE), BF16),
            jax.ShapeDtypeStruct((2, 32, LANE), F32),
            jax.ShapeDtypeStruct((2, BLOCKS, 384), BF16),
            jax.ShapeDtypeStruct((3, 32, LANE), F32),
        ),
        in_specs=[HBM] * 7,
        out_specs=(VMEM,) * 4,
        scratch_shapes=[
            pltpu.VMEM((1, BLOCKS), jnp.int32),
            pltpu.VMEM((16, BLOCKS), jnp.int32),
            pltpu.VMEM((BLOCKS, LANE), jnp.int32),
            pltpu.VMEM((BLOCKS, BLOCK), BF16),
            pltpu.VMEM((8, BLOCKS, 256), F32),
            pltpu.SemaphoreType.DMA((7,)),
        ],
        compiler_params=ROOM,
        name="rotate",
    )(*(pltpu.with_memory_space_constraint(each, pltpu.HBM) for each in inputs))
    got = lax.all_gather(halves[0].reshape(1536, LANE), "core", axis=0, tiled=True).reshape(2, 16, 96, LANE)
    other = lax.dynamic_index_in_dim(got, 1 - core, 0, keepdims=False)
    part = (halves[1].astype(F32) + other.astype(F32)).astype(BF16)
    got = lax.all_to_all(part.reshape(4, 384, LANE), "x", 0, 0, tiled=True)

    def local(kernel, name, out_shape, *operands):
        return pl.pallas_call(
            kernel,
            out_shape=out_shape,
            in_specs=[VMEM] * len(operands),
            out_specs=jax.tree.map(lambda _: VMEM, out_shape),
            compiler_params=ROOM,
            name=name,
        )(*operands)

    sent = local(x_sum_kernel, "x_sum", jax.ShapeDtypeStruct((12, 32, LANE), BF16), got)
    sent, state = lax.optimization_barrier((sent, state))
    lend = []
    for x in range(4):
        for y in (x, x + 4):
            for up, right in ((2, 0), (1, 1), (-1, -1), (0, 2)):
                source, target = (y, (x + right) % 4), ((y + up) % 8, x)
                lend.append(tuple((row % 4 * 2 + row // 4) * 4 + column for row, column in (source, target)))
    lent = lax.ppermute(state, ("y_lo", "y_hi", "x"), lend)
    got = lax.all_to_all(sent, "z", 0, 0, tiled=True)
    sent = local(z_sum_kernel, "z_sum", jax.ShapeDtypeStruct((8, 32, LANE), F32), got)
    got = lax.all_to_all(sent, ("y_lo", "y_hi"), 0, 0, tiled=True)
    shapes = (jax.ShapeDtypeStruct((12, 32, LANE), BF16), jax.ShapeDtypeStruct((3, 32, LANE), BF16))
    sent, terms = local(adam_kernel, "adam", shapes, got, signs, lent)
    got = lax.all_to_all(sent, "z", 0, 0, tiled=True)
    sent = local(repeat_kernel, "repeat", jax.ShapeDtypeStruct((4, 480, LANE), BF16), got, terms)
    got = lax.all_to_all(sent, "x", 0, 0, tiled=True)
    got = lax.all_gather(got.reshape(1920, LANE), "core", axis=0, tiled=True).reshape(2, 4, 480, LANE)

    kept = jax.ShapeDtypeStruct((32, LANE), F32)
    params, *news = pl.pallas_call(
        params_kernel,
        out_shape=(jax.ShapeDtypeStruct((BLOCKS, BLOCK), BF16), kept, kept, kept),
        in_specs=[VMEM] * 4,
        out_specs=(HBM,) * 4,
        scratch_shapes=[
            pltpu.VMEM((BLOCKS, BLOCK), BF16),
            pltpu.VMEM((3, 32, LANE), F32),
            pltpu.SemaphoreType.DMA((7,)),
        ],
        compiler_params=ROOM,
        name="params",
    )(place, got, signs, state)
    return *(by_slot(new) for new in news), params


def solution(mesh):
    fine = Mesh(np.asarray(mesh.devices).reshape(SIZES), AXES)
    group = ("y_lo", "z", "core")
    placed = (
        P(AXES, None, None),
        P(),
        P(),
        P(),
        P(group, None),
        P(group, None),
        P(group, None),
    )
    return jax.shard_map(
        on_device,
        mesh=fine,
        in_specs=placed,
        out_specs=(P(group, None), P(group, None), P(group, None), P()),
        check_vma=False,
    )
```

```python
import math

import jax
import jax.numpy as jnp
import numpy as np
from jax import lax
from jax.experimental import pallas as pl
from jax.experimental.pallas import tpu as pltpu
from jax.sharding import Mesh, PartitionSpec as P

beta_one = 0.9
beta_two = 0.95
first_fix = 1.0 - math.exp(100.0 * math.log(0.9))
second_fix = 1.0 - math.exp(100.0 * math.log(0.95))
learn_rate = 0.25
weight_decay = 0.1
epsilon = 1e-08

AXES = ("y_lo", "z", "core", "y_hi", "x")
SIZES = (4, 12, 2, 2, 4)
BLOCKS = 192
BLOCK = 2048
LANE = 128
INV_ROOT = 1.0 / math.sqrt(BLOCK)
F32 = jnp.float32
BF16 = jnp.bfloat16


def iota(shape, axis):
    return lax.broadcasted_iota(jnp.int32, shape, axis)


def parity_sign(both, bits):
    for shift in bits:
        both = both ^ jnp.right_shift(both, shift)
    return (1 - 2 * (both & 1)).astype(F32)


def rotate_kernel(
    order_hbm, rows_hbm, cols_hbm, grad_hbm, master_hbm, first_hbm, second_hbm,
    out_ref, signs_ref, place_ref, state_ref, order_ref, rows_ref, cols_ref, grad_ref, mixed_ref, sems
):
    small = [
        pltpu.make_async_copy(order_hbm, order_ref, sems.at[0]),
        pltpu.make_async_copy(rows_hbm, rows_ref, sems.at[1]),
        pltpu.make_async_copy(cols_hbm, cols_ref, sems.at[2]),
    ]
    large = pltpu.make_async_copy(grad_hbm, grad_ref, sems.at[3])
    states = [
        pltpu.make_async_copy(each, state_ref.at[i], sems.at[4 + i])
        for i, each in enumerate((master_hbm, first_hbm, second_hbm))
    ]
    for copy in small + [large] + states:
        copy.start()
    core = lax.axis_index("core")
    row = iota((BLOCKS, BLOCKS), 0)
    lane = iota((BLOCKS, BLOCKS), 1)
    half = (row >= 96).astype(jnp.int32)
    place = row - 96 * half
    y_lo = sum((place >= bound).astype(jnp.int32) for bound in (24, 48, 72))
    z = jnp.right_shift(place - 24 * y_lo, 1)
    owner = jnp.where(half == 1, core, 1 - core)
    slot = ((y_lo * 12 + z) * 2 + owner) * 2 + (place & 1)
    table = parity_sign(iota((256, 256), 0) & iota((256, 256), 1), (4, 2, 1)).astype(BF16)
    spread = jnp.where(iota((32, 16), 1) == jnp.right_shift(iota((32, 16), 0), 1), 1.0, 0.0).astype(BF16)
    wide_lane = iota((BLOCKS, 384), 1)
    core_of = (wide_lane >= 192).astype(jnp.int32)
    rest = wide_lane - 192 * core_of
    y_of = sum((rest >= bound).astype(jnp.int32) for bound in (48, 96, 144))
    rest = rest - 48 * y_of
    parity = (rest >= 24).astype(jnp.int32)
    rest = rest - 24 * parity
    slot_of = ((y_of * 12 + jnp.right_shift(rest, 1)) * 2 + core_of) * 2 + (rest & 1)
    wide_row = iota((BLOCKS, 384), 0)
    scatter = jnp.where(wide_row == slot_of, 1.0, 0.0).astype(BF16)
    for copy in small:
        copy.wait()
    order = order_ref[...].astype(F32)
    block = jnp.sum(jnp.where(slot == lane, order, 0.0), axis=1, keepdims=True)
    pick = jnp.where(block == lane.astype(F32), 1.0, 0.0).astype(BF16)
    row_bits = (2 * rows_ref[...] - 1).astype(F32).astype(BF16)
    col_bits = (2 * cols_ref[...] - 1).astype(F32).astype(BF16)
    row_signs = lax.dot_general(pick, row_bits, (((1,), (1,)), ((), ())), preferred_element_type=F32)
    col_signs = jnp.dot(pick, col_bits, preferred_element_type=F32)

    wide = jnp.dot(spread, row_bits, preferred_element_type=F32)
    for i, axis in enumerate(("x", "y_lo")):
        own = ((lax.axis_index(axis) * 12 + lax.axis_index("z")) * 2 + core) * 2
        wanted = iota((32, BLOCKS), 1) == own + (iota((32, BLOCKS), 0) & 1)
        own_block = jnp.sum(jnp.where(wanted, order, 0.0), axis=1, keepdims=True)
        own_pick = jnp.where(own_block == iota((32, BLOCKS), 1).astype(F32), 1.0, 0.0)
        own_rows = jnp.sum(wide * own_pick, axis=1, keepdims=True)
        signs_ref[i] = own_rows * jnp.dot(own_pick.astype(BF16), col_bits, preferred_element_type=F32)
    orders = jnp.broadcast_to(order, (8, BLOCKS)).astype(BF16)
    placed = jnp.dot(orders, scatter, preferred_element_type=F32)[0:1]
    match = wide_row.astype(F32) == placed
    for i in range(2):
        place_ref[i] = jnp.where(match & (parity == i), 1.0, 0.0).astype(BF16)

    large.wait()
    picked = jnp.dot(pick, grad_ref[...], preferred_element_type=F32)
    signed = []
    for k in range(8):
        pair = [
            picked[:, a * LANE : (a + 1) * LANE] * col_signs * row_signs[:, a : a + 1] for a in (2 * k, 2 * k + 1)
        ]
        signed.append(jnp.concatenate(pair, axis=1).astype(BF16))
    product = jnp.dot(jnp.concatenate(signed, axis=0), table, preferred_element_type=F32)
    for k in range(8):
        mixed_ref[k] = product[k * BLOCKS : (k + 1) * BLOCKS]
    for start in range(0, BLOCKS, 24):
        mixed = [mixed_ref[k, start : start + 24] for k in range(8)]
        for span in (1, 2, 4):
            for k in range(8):
                if not k & span:
                    low, high = mixed[k], mixed[k + span]
                    mixed[k], mixed[k + span] = low + high, low - high
        for x in range(4):
            pair = mixed[2 * x], mixed[2 * x + 1]
            rows = [part[:, c : c + LANE] * INV_ROOT for part in pair for c in (0, LANE)]
            out_ref[start // 96, (start % 96) // 24 * 4 + x] = jnp.concatenate(rows, axis=0).astype(BF16)
    for copy in states:
        copy.wait()


def x_sum_kernel(got_ref, out_ref):
    total = got_ref[0].astype(F32)
    for x in range(1, 4):
        total = total + got_ref[x].astype(F32)
    for z in range(12):
        rows = [total[24 * a + 2 * z : 24 * a + 2 * z + 2] for a in range(16)]
        out_ref[z] = jnp.concatenate(rows, axis=0).astype(BF16)


def z_sum_kernel(got_ref, out_ref):
    total = got_ref[0].astype(F32)
    for z in range(1, 12):
        total = total + got_ref[z].astype(F32)
    for y in range(8):
        out_ref[y] = total


def adam_step(gradient, signs, master, first, second):
    new_first = beta_one * first + (1.0 - beta_one) * gradient
    new_second = beta_two * second + (1.0 - beta_two) * gradient * gradient
    update = new_first / first_fix / (jnp.sqrt(new_second / second_fix) + epsilon)
    row, col = iota((32, 32), 0), iota((32, 32), 1)
    same = ((row ^ col) & 1) == 0
    sub = jnp.where(same, parity_sign(jnp.right_shift(row & col, 1), (2, 1)), 0.0)
    table = parity_sign(iota((LANE, LANE), 0) & iota((LANE, LANE), 1), (4, 2, 1))
    restored = jnp.dot(sub, update, precision=lax.Precision.HIGHEST, preferred_element_type=F32)
    restored = jnp.dot(restored, table, precision=lax.Precision.HIGHEST, preferred_element_type=F32)
    restored = restored * INV_ROOT * signs
    new_master = master - learn_rate * (restored + weight_decay * master)
    return new_master, new_first, new_second


def adam_kernel(got_ref, signs_ref, state_ref, sent_ref, terms_ref):
    gradient = got_ref[0]
    for y in range(1, 8):
        gradient = gradient + got_ref[y]
    new_master, _, _ = adam_step(gradient, signs_ref[0], state_ref[0], state_ref[1], state_ref[2])
    mine = new_master.astype(BF16)
    for z in range(12):
        sent_ref[z] = mine
    for i in range(3):
        term = gradient.astype(BF16)
        terms_ref[i] = term
        gradient = gradient - term.astype(F32)


def repeat_kernel(got_ref, terms_ref, out_ref):
    wide = [got_ref[z].astype(F32) for z in range(12)]
    for pair in range(8):
        rows = [wide[z][2 * a : 2 * a + 2] for a in (2 * pair, 2 * pair + 1) for z in range(12)]
        piece = jnp.concatenate(rows, axis=0).astype(BF16)
        for x in range(4):
            out_ref[x, 48 * pair : 48 * pair + 48] = piece
    for i in range(3):
        for x in range(4):
            out_ref[x, 384 + 32 * i : 416 + 32 * i] = terms_ref[i]


def params_kernel(
    place_ref, got_ref, signs_ref, state_ref, out_hbm, master_hbm, first_hbm, second_hbm, out_ref, new_ref, sems
):
    rows = jnp.concatenate(
        [
            jnp.concatenate(
                [got_ref[c, y, 48 * pair : 48 * pair + 48] for c in range(2) for y in range(4)], axis=0
            )
            for pair in range(8)
        ],
        axis=1,
    )
    copies = []
    for quarter in range(4):
        part = rows[:, 256 * quarter : 256 * quarter + 256]
        for i in range(2):
            placed = jnp.dot(place_ref[i], part, preferred_element_type=F32).astype(BF16)
            for k in range(2):
                column = (4 * quarter + 2 * k + i) * LANE
                out_ref[:, column : column + LANE] = placed[:, k * LANE : (k + 1) * LANE]
        columns = slice(512 * quarter, 512 * quarter + 512)
        copies.append(pltpu.make_async_copy(out_ref.at[:, columns], out_hbm.at[:, columns], sems.at[quarter]))
        copies[-1].start()
    terms = got_ref.at[lax.axis_index("core"), lax.axis_index("y_lo")]
    gradient = terms[384:416].astype(F32) + terms[416:448].astype(F32) + terms[448:480].astype(F32)
    news = adam_step(gradient, signs_ref[1], state_ref[0], state_ref[1], state_ref[2])
    for i, target in enumerate((master_hbm, first_hbm, second_hbm)):
        new_ref[i] = news[i]
        copies.append(pltpu.make_async_copy(new_ref.at[i], target, sems.at[4 + i]))
        copies[-1].start()
    for copy in copies:
        copy.wait()


VMEM = pl.BlockSpec(memory_space=pltpu.VMEM)
HBM = pl.BlockSpec(memory_space=pltpu.HBM)
ROOM = pltpu.CompilerParams(vmem_limit_bytes=32 * 1024 * 1024)


def on_device(grads, sign_rows, sign_cols, block_order, master, first_moment, second_moment):
    core = lax.axis_index("core")
    order_row = block_order.reshape(1, BLOCKS)
    rows_t = sign_rows.T

    def by_row(value):
        return value.reshape(2, 16, LANE).transpose(1, 0, 2).reshape(32, LANE)

    def by_slot(value):
        return value.reshape(16, 2, LANE).transpose(1, 0, 2).reshape(2, BLOCK)

    inputs = order_row, rows_t, sign_cols, grads[0], by_row(master), by_row(first_moment), by_row(second_moment)
    halves, signs, place, state = pl.pallas_call(
        rotate_kernel,
        out_shape=(
            jax.ShapeDtypeStruct((2, 16, 96, LANE), BF16),
            jax.ShapeDtypeStruct((2, 32, LANE), F32),
            jax.ShapeDtypeStruct((2, BLOCKS, 384), BF16),
            jax.ShapeDtypeStruct((3, 32, LANE), F32),
        ),
        in_specs=[HBM] * 7,
        out_specs=(VMEM,) * 4,
        scratch_shapes=[
            pltpu.VMEM((1, BLOCKS), jnp.int32),
            pltpu.VMEM((16, BLOCKS), jnp.int32),
            pltpu.VMEM((BLOCKS, LANE), jnp.int32),
            pltpu.VMEM((BLOCKS, BLOCK), BF16),
            pltpu.VMEM((8, BLOCKS, 256), F32),
            pltpu.SemaphoreType.DMA((7,)),
        ],
        compiler_params=ROOM,
        name="rotate",
    )(*(pltpu.with_memory_space_constraint(each, pltpu.HBM) for each in inputs))
    got = lax.all_gather(halves[0].reshape(1536, LANE), "core", axis=0, tiled=True).reshape(2, 16, 96, LANE)
    other = lax.dynamic_index_in_dim(got, 1 - core, 0, keepdims=False)
    part = (halves[1].astype(F32) + other.astype(F32)).astype(BF16)
    got = lax.all_to_all(part.reshape(4, 384, LANE), "x", 0, 0, tiled=True)

    def local(kernel, name, out_shape, *operands):
        return pl.pallas_call(
            kernel,
            out_shape=out_shape,
            in_specs=[VMEM] * len(operands),
            out_specs=jax.tree.map(lambda _: VMEM, out_shape),
            compiler_params=ROOM,
            name=name,
        )(*operands)

    sent = local(x_sum_kernel, "x_sum", jax.ShapeDtypeStruct((12, 32, LANE), BF16), got)
    sent, state = lax.optimization_barrier((sent, state))
    lend = []
    for x in range(4):
        for y in (x, x + 4):
            for up, right in ((2, 0), (1, 1), (-1, -1), (0, 2)):
                source, target = (y, (x + right) % 4), ((y + up) % 8, x)
                lend.append(tuple((row % 4 * 2 + row // 4) * 4 + column for row, column in (source, target)))
    lent = lax.ppermute(state, ("y_lo", "y_hi", "x"), lend)
    got = lax.all_to_all(sent, "z", 0, 0, tiled=True)
    sent = local(z_sum_kernel, "z_sum", jax.ShapeDtypeStruct((8, 32, LANE), F32), got)
    sent, lent = lax.optimization_barrier((sent, lent))
    got = lax.all_to_all(sent, ("y_lo", "y_hi"), 0, 0, tiled=True)
    shapes = (jax.ShapeDtypeStruct((12, 32, LANE), BF16), jax.ShapeDtypeStruct((3, 32, LANE), BF16))
    sent, terms = local(adam_kernel, "adam", shapes, got, signs, lent)
    got = lax.all_to_all(sent, "z", 0, 0, tiled=True)
    sent = local(repeat_kernel, "repeat", jax.ShapeDtypeStruct((4, 480, LANE), BF16), got, terms)
    got = lax.all_to_all(sent, "x", 0, 0, tiled=True)
    got = lax.all_gather(got.reshape(1920, LANE), "core", axis=0, tiled=True).reshape(2, 4, 480, LANE)

    kept = jax.ShapeDtypeStruct((32, LANE), F32)
    params, *news = pl.pallas_call(
        params_kernel,
        out_shape=(jax.ShapeDtypeStruct((BLOCKS, BLOCK), BF16), kept, kept, kept),
        in_specs=[VMEM] * 4,
        out_specs=(HBM,) * 4,
        scratch_shapes=[
            pltpu.VMEM((BLOCKS, BLOCK), BF16),
            pltpu.VMEM((3, 32, LANE), F32),
            pltpu.SemaphoreType.DMA((7,)),
        ],
        compiler_params=ROOM,
        name="params",
    )(place, got, signs, state)
    return *(by_slot(new) for new in news), params


def solution(mesh):
    fine = Mesh(np.asarray(mesh.devices).reshape(SIZES), AXES)
    group = ("y_lo", "z", "core")
    placed = (
        P(AXES, None, None),
        P(),
        P(),
        P(),
        P(group, None),
        P(group, None),
        P(group, None),
    )
    return jax.shard_map(
        on_device,
        mesh=fine,
        in_specs=placed,
        out_specs=(P(group, None), P(group, None), P(group, None), P()),
        check_vma=False,
    )
```
